32 devices in a mesh: group: 2 (over x), freq: 16 (over z, y, core).
Axes of the slice: x: 2, y: 2, z: 4, core: 2. Of those that a mesh axis runs over, the one named last changes fastest.
Arguments:
- traces: bfloat16 [512, 256, 256], P(('group', 'freq')), parts along dimension 0, may hold values from -6 to 6
- velocity: bfloat16 [32, 256, 256], P(('group', 'freq')), parts along dimension 0, may hold values from 1 to 2
- poly_coef: float32 [2, 10, 4], replicated, may hold values from -0.6 to 0.6
- freq_slot: int32 [16], replicated, may hold values from 0 to 15, each once
- depth_owner: int32 [8], P('group'), parts along dimension 0, may hold values from 0 to 15, as said below
Outputs:
- depth_image: float32 [4, 512, 256], P(None, ('group', 'freq')), parts along dimension 1
- wavefield: float32 [2, 32, 256, 256], P(None, ('group', 'freq')), parts along dimension 1
The draws below stay inside these ranges and needn't reach their ends.
There are 2 independent parts, one for each index of `group`. The reference program is written for one: setup_inputs(seed, part) draws one part's arguments, and reference() takes and returns one part's arrays. A program takes and returns all parts, laid end to end along the dimension named above; an argument that names none is the same for every part. Nothing has to cross between parts.
Inputs may be any that keep to these rules, and one draw needn't show every extreme that they name: `freq_slot`: each slot holds a different frequency index. `depth_owner`: the 4 entries are different.
All inputs are finite; a program needn't handle non-finite values.
Results may differ from the reference program's by a relative error of at most 0.0023.
Values may be sent and summed in bfloat16 or wider, within the bound.
No kernel may reach another device: no remote copies, remote signals or barrier semaphores. Data moves between devices by JAX's collectives and lax.ppermute only.
A program may use at most 128 MiB of HBM per device.

```python
import math
import jax
import jax.numpy as jnp
from jax import lax

NX = 256
NY = 256
NT = 256
NTERM = 10
NPOW = 4
NZ = 4
NF = 16
VSLICES = 16


def draw_depth_owner(key, part):
    middle_owners = jax.random.permutation(jax.random.fold_in(key, 11), VSLICES - 2)[:NZ - 2] + 1
    chosen = jnp.concatenate([jnp.array([0, VSLICES - 1], jnp.int32), middle_owners.astype(jnp.int32)])
    shuffle = jax.random.permutation(jax.random.fold_in(key, 12), NZ)
    return chosen[shuffle].astype(jnp.int32)


def shard_levels(rng, shape, pieces, low, top_value):
    factor_of, own = 1.0, jax.random.fold_in(rng, 6)
    for position, parts in pieces:
        draws = jnp.exp(jax.random.uniform(jax.random.fold_in(own, position), (parts,), jnp.float32, low / len(pieces), top_value / len(pieces)))
        factor_of = factor_of * jnp.repeat(draws, shape[position] // parts).reshape([-1 if axis == position else 1 for axis in range(len(shape))])
    return factor_of


def gaussian(stream_key, extent, width, most, pieces=(), kind=jnp.bfloat16):
    entries = jax.random.normal(stream_key, extent, jnp.float32) * width
    if len(pieces) > 0:
        entries = shard_levels(stream_key, extent, pieces, -0.22, 0.18) * entries
    return jnp.clip(entries, min=-most, max=most).astype(kind)


def setup_inputs(seed: int = 0, part: int = 0) -> dict:
    arg_keys = jax.random.split(jax.random.key(seed), 6)
    part_keys = jax.random.split(jax.random.fold_in(arg_keys[5], part), 6)
    traces = gaussian(part_keys[0], (NX, NY, NT), 1.0, 6.0, ((0, 16),))
    velocity = jnp.clip(1.0 + 1.0 * jax.random.uniform(part_keys[1], (VSLICES, NX, NY), jnp.float32) ** shard_levels(part_keys[1], (VSLICES, NX, NY), ((0, 16),), -0.2, 0.2), 1.0, 2.0).astype(jnp.bfloat16)
    poly_coef = gaussian(arg_keys[2], (2, NTERM, NPOW), 0.1, 0.6, (), jnp.float32)
    freq_slot = jax.random.permutation(arg_keys[3], NF).astype(jnp.int32)
    depth_owner = draw_depth_owner(jax.random.fold_in(jax.random.fold_in(arg_keys[5], part), 71), part)
    return {"traces": traces, "velocity": velocity, "poly_coef": poly_coef, "freq_slot": freq_slot, "depth_owner": depth_owner}


def mcclellan(values):
    padded = jnp.pad(values, [(0, 0)] * (values.ndim - 2) + [(1, 1), (1, 1)])
    row_sum = padded[..., :-2, :] + 2.0 * padded[..., 1:-1, :] + padded[..., 2:, :]
    smoothed = row_sum[..., :-2] + 2.0 * row_sum[..., 1:-1] + row_sum[..., 2:]
    return smoothed * 0.125 - values

def coefficient_pair(poly_coef, order_index, powers):
    real_part = poly_coef[0, order_index, 0] * powers[0]
    imag_part = poly_coef[1, order_index, 0] * powers[0]
    for power_index in range(1, len(powers)):
        real_part = real_part + poly_coef[0, order_index, power_index] * powers[power_index]
        imag_part = imag_part + poly_coef[1, order_index, power_index] * powers[power_index]
    return (real_part, imag_part)

def accumulate(summed, real_part, imag_part, term):
    new_real = summed[0] + real_part * term[0] - imag_part * term[1]
    new_imag = summed[1] + real_part * term[1] + imag_part * term[0]
    return jnp.stack([new_real, new_imag])

def reference(traces, velocity, poly_coef, freq_slot, depth_owner):
    freq_bin = (freq_slot + 1).astype(jnp.int32)
    sample_index = jnp.arange(NT, dtype=jnp.int32)
    phase_int = freq_bin[:, None] * sample_index[None, :] % NT
    phases = phase_int.astype(jnp.float32) * (2.0 * math.pi / NT)
    dft_table = (jnp.stack([jnp.cos(phases), -jnp.sin(phases)]) / math.sqrt(NT)).astype(jnp.bfloat16)
    wavefield = jnp.einsum('cft,xyt->cfxy', dft_table.astype(jnp.float32), traces.astype(jnp.float32), precision=lax.Precision.HIGHEST)
    freq_value = freq_bin.astype(jnp.float32)
    image_terms = []
    for depth_index in range(NZ):
        speed = velocity[depth_owner[depth_index]].astype(jnp.float32)
        slowness = freq_value[:, None, None] / (NF * speed[None, :, :])
        powers = [jnp.ones_like(slowness)]
        for power_index in range(1, NPOW):
            powers.append(powers[-1] * slowness)
        term_prev = wavefield
        real_part, imag_part = coefficient_pair(poly_coef, 0, powers)
        summed = accumulate(jnp.zeros_like(wavefield), real_part, imag_part, term_prev)
        term_now = mcclellan(wavefield)
        real_part, imag_part = coefficient_pair(poly_coef, 1, powers)
        summed = accumulate(summed, real_part, imag_part, term_now)
        for order_index in range(2, NTERM):
            term_next = 2.0 * mcclellan(term_now) - term_prev
            real_part, imag_part = coefficient_pair(poly_coef, order_index, powers)
            summed = accumulate(summed, real_part, imag_part, term_next)
            term_prev, term_now = (term_now, term_next)
        wavefield = summed
        image_terms.append(lax.optimization_barrier(jnp.sum(wavefield[0], axis=0)) / math.sqrt(NF))
    return (jnp.stack(image_terms), wavefield)
```

```python
import math

import jax
import jax.numpy as jnp
import numpy as np
from jax import lax
from jax.experimental import pallas as pl
from jax.experimental.pallas import tpu as pltpu
from jax.sharding import PartitionSpec as P

SUBLANES = 8


def newton_nodes(count):
    points = list(np.cos(np.pi * (2 * np.arange(count) + 1) / (2 * count)))
    ordered = [points.pop(0)]
    while points:
        spread = [np.prod([abs(p - q) for q in ordered]) for p in points]
        ordered.append(points.pop(int(np.argmax(spread))))
    return np.array(ordered)


def basis_change(term_count):
    nodes = newton_nodes(max(term_count - 1, 1))
    table = np.zeros((term_count, term_count))
    table[0, 0] = 1.0

    def times_g(row):
        out = np.zeros_like(row)
        for m in range(term_count):
            if row[m] != 0.0:
                out[m] += nodes[m] * row[m]
                out[m + 1] += row[m] / 8.0
        return out

    if term_count > 1:
        table[1] = times_g(table[0])
    for k in range(2, term_count):
        table[k] = 2.0 * times_g(table[k - 1]) - table[k - 2]
    return table, nodes


def extrapolate_kernel(
    coef_ref, node_ref, core_ref, start_ref, mine_ref, other_ref, image_ref, field_ref,
    terms, summed, slow, flat, *, term_count, power_count, depth_count, image_scale,
):
    rows = start_ref.shape[1] // SUBLANES
    half = start_ref.shape[2] // 2
    held = mine_ref.shape[0]
    lane = lax.broadcasted_iota(jnp.int32, (SUBLANES, half), 1)
    sub = lax.broadcasted_iota(jnp.int32, (SUBLANES, 2 * half), 0)
    first_lane, last_lane = lane == 0, lane == half - 1
    first_sub, last_sub = sub == 0, sub == SUBLANES - 1

    def strided(m):
        return pl.ds(m, SUBLANES, stride=rows)

    def edges(slot):
        for c in range(2):
            above = pltpu.roll(terms[slot, c, rows], 1, 0)
            below = pltpu.roll(terms[slot, c, 1], SUBLANES - 1, 0)
            terms[slot, c, 0] = jnp.where(first_sub, 0.0, above)
            terms[slot, c, rows + 1] = jnp.where(last_sub, 0.0, below)

    def spread_rows(values):
        flat[0], flat[1] = values[:, :half], values[:, half:]
        return [
            jnp.concatenate([flat[0, strided(m), :], flat[1, strided(m), :]], axis=1) for m in range(rows)
        ]

    def gather_rows(values):
        for m in range(rows):
            flat[0, strided(m), :] = values[m][:, :half]
            flat[1, strided(m), :] = values[m][:, half:]
        return jnp.concatenate([flat[0], flat[1]], axis=1)

    for c in range(2):
        for m, value in enumerate(spread_rows(start_ref[c])):
            terms[0, c, m + 1] = value

    def smooth(values):
        low, high = values[:, :half], values[:, half:]
        roll_low, roll_high = pltpu.roll(low, 1, 1), pltpu.roll(high, 1, 1)
        sum_low = low + jnp.where(first_lane, 0.0, roll_low)
        sum_high = high + jnp.where(first_lane, roll_low, roll_high)
        roll_low, roll_high = pltpu.roll(sum_low, half - 1, 1), pltpu.roll(sum_high, half - 1, 1)
        out_low = sum_low + jnp.where(last_lane, roll_high, roll_low)
        out_high = sum_high + jnp.where(last_lane, high, roll_high)
        return jnp.concatenate([out_low, out_high], axis=1)

    def coefficients(order, s):
        out = []
        for c in range(2):
            value = coef_ref[c, order, power_count - 1]
            for j in range(power_count - 2, -1, -1):
                value = value * s + coef_ref[c, order, j]
            out.append(value)
        return out

    def depth_step(z, carry):
        edges(0)

        def load_slow(ref):
            for m, value in enumerate(spread_rows(ref[z % held])):
                slow[m] = 1.0 / value

        @pl.when(z // held == core_ref[0])
        def _():
            load_slow(mine_ref)

        @pl.when(z // held != core_ref[0])
        def _():
            load_slow(other_ref)

        for m in range(rows):
            re, im = coefficients(0, slow[m])
            a, b = terms[0, 0, m + 1], terms[0, 1, m + 1]
            summed[0, m] = re * a - im * b
            summed[1, m] = re * b + im * a

        def order_step(order, carry):
            source = lax.rem(order + 1, 2)
            target = lax.rem(order, 2)
            node = node_ref[order - 1]
            pair = [[None] * (rows + 2) for _ in range(2)]
            value = [[None] * (rows + 2) for _ in range(2)]
            for c in range(2):
                value[c][0] = terms[source, c, 0]
                value[c][1] = terms[source, c, 1]
                pair[c][0] = value[c][0] + value[c][1]
            for m in range(rows):
                new = []
                for c in range(2):
                    value[c][m + 2] = terms[source, c, m + 2]
                    pair[c][m + 1] = value[c][m + 1] + value[c][m + 2]
                    stencil = smooth(pair[c][m] + pair[c][m + 1])
                    new.append(stencil - node * value[c][m + 1])
                    terms[target, c, m + 1] = new[c]
                re, im = coefficients(order, slow[m])
                summed[0, m] = summed[0, m] + (re * new[0] - im * new[1])
                summed[1, m] = summed[1, m] + (re * new[1] + im * new[0])
            edges(target)
            return carry

        lax.fori_loop(1, term_count, order_step, 0)
        for m in range(rows):
            terms[0, 0, m + 1] = summed[0, m]
            terms[0, 1, m + 1] = summed[1, m]
        image_ref[z] = gather_rows([summed[0, m] * image_scale for m in range(rows)])
        return carry

    lax.fori_loop(0, depth_count, depth_step, 0)
    for c in range(2):
        field_ref[c] = gather_rows([summed[c, m] for m in range(rows)])


def extrapolate(coefs, nodes, core, start, mine, other, depth_count, image_scale):
    _, nx, ny = start.shape
    rows = nx // SUBLANES
    _, term_count, power_count = coefs.shape

    def kernel(*refs):
        extrapolate_kernel(
            *refs,
            term_count=term_count,
            power_count=power_count,
            depth_count=depth_count,
            image_scale=image_scale,
        )

    smem = pl.BlockSpec(memory_space=pltpu.SMEM)
    vmem = pl.BlockSpec(memory_space=pltpu.VMEM)
    return pl.pallas_call(
        kernel,
        out_shape=(
            jax.ShapeDtypeStruct((depth_count, nx, ny), jnp.float32),
            jax.ShapeDtypeStruct((2, nx, ny), jnp.float32),
        ),
        in_specs=[smem, smem, smem, vmem, vmem, vmem],
        out_specs=(vmem, vmem),
        scratch_shapes=[
            pltpu.VMEM((2, 2, rows + 2, SUBLANES, ny), jnp.float32),
            pltpu.VMEM((2, rows, SUBLANES, ny), jnp.float32),
            pltpu.VMEM((rows, SUBLANES, ny), jnp.float32),
            pltpu.VMEM((2, nx, ny // 2), jnp.float32),
        ],
        compiler_params=pltpu.CompilerParams(vmem_limit_bytes=32 * 1024 * 1024),
        cost_estimate=pl.CostEstimate(
            flops=depth_count * term_count * 40 * nx * ny, bytes_accessed=16 * nx * ny, transcendentals=0
        ),
        name="depth_steps",
    )(coefs, nodes, core, start, mine, other)


def swap_cores(array, count):
    return lax.ppermute(array, "freq", [(i, i ^ 1) for i in range(count)])


def on_device(traces, velocity, poly_coef, freq_slot, depth_owner):
    devices = lax.axis_size("freq")
    total_freq = freq_slot.shape[0]
    local_x, ny, sample_count = traces.shape
    nx = devices * local_x
    depth_count = depth_owner.shape[0]
    term_count, power_count = poly_coef.shape[1:]
    me = lax.axis_index("freq")
    core = me % 2

    by_rows = lax.all_to_all(
        velocity.reshape(devices, local_x, ny), "freq", split_axis=0, concat_axis=0, tiled=True
    )
    chosen = jnp.stack(
        [lax.dynamic_index_in_dim(by_rows, depth_owner[z], 0, keepdims=False) for z in range(depth_count)]
    ).astype(jnp.float16)

    freq_bin = freq_slot + 1
    sample_index = jnp.arange(sample_count, dtype=jnp.int32)
    phase_int = freq_bin[:, None] * sample_index[None, :] % sample_count
    phases = phase_int.astype(jnp.float32) * (2.0 * math.pi / sample_count)
    dft_table = (jnp.stack([jnp.cos(phases), -jnp.sin(phases)]) / math.sqrt(sample_count)).astype(
        jnp.bfloat16
    )
    spectra = jnp.einsum("cft,xyt->fcxy", dft_table, traces, preferred_element_type=jnp.float32)
    spectra = (spectra * 512.0).astype(jnp.float16)

    held = depth_count // 2
    halves = jnp.broadcast_to(
        chosen.reshape(1, 2, held, local_x, ny), (devices // 2, 2, held, local_x, ny)
    ).reshape(devices, held, local_x, ny)
    received = lax.all_to_all(
        jnp.concatenate([spectra, halves], axis=1), "freq", split_axis=0, concat_axis=0, tiled=True
    )
    gathered = received.transpose(1, 0, 2, 3).reshape(2 + held, nx, ny)
    start = gathered[:2].astype(jnp.float32) * (1.0 / 512.0)
    mine_half = gathered[2:]
    other_half = swap_cores(mine_half, devices)
    mine, other = mine_half.astype(jnp.float32), other_half.astype(jnp.float32)

    table, nodes = basis_change(term_count)
    freq_value = lax.dynamic_index_in_dim(freq_bin, me, 0, keepdims=False).astype(jnp.float32)
    scale = freq_value / total_freq
    powers = jnp.stack([scale**j for j in range(power_count)])
    coefs = (
        jnp.einsum("ckj,km->cmj", poly_coef, jnp.asarray(table, jnp.float32), precision=lax.Precision.HIGHEST)
        * powers
    )
    images, wavefield = extrapolate(
        coefs,
        jnp.asarray(8.0 * (1.0 + nodes), jnp.float32),
        core.astype(jnp.int32).reshape(1),
        start,
        mine,
        other,
        depth_count,
        1.0 / math.sqrt(total_freq),
    )

    by_core = images.reshape(depth_count, devices // 2, 2, local_x, ny)
    keep = lax.dynamic_index_in_dim(by_core, core, 2, keepdims=False)
    send = lax.dynamic_index_in_dim(by_core, 1 - core, 2, keepdims=False)
    pair_sum = keep + swap_cores(send, devices)
    same_core = [[i for i in range(devices) if i % 2 == c] for c in range(2)]
    shares = lax.all_to_all(
        pair_sum.transpose(1, 0, 2, 3),
        "freq",
        split_axis=0,
        concat_axis=0,
        tiled=True,
        axis_index_groups=same_core,
    )
    return (jnp.sum(shares, axis=0), wavefield[:, None])


def solution(mesh):
    return jax.shard_map(
        on_device,
        mesh=mesh,
        in_specs=(
            P(("group", "freq"), None, None),
            P(("group", "freq"), None, None),
            P(),
            P(),
            P("group"),
        ),
        out_specs=(P(None, ("group", "freq"), None), P(None, ("group", "freq"), None, None)),
        check_vma=False,
    )
```

```python
import math

import jax
import jax.numpy as jnp
import numpy as np
from jax import lax
from jax.experimental import pallas as pl
from jax.experimental.pallas import tpu as pltpu
from jax.sharding import PartitionSpec as P

def sine_transform(size):
    index = np.arange(1, size + 1)
    matrix = np.sqrt(2.0 / (size + 1)) * np.sin(np.pi * np.outer(index, index) / (size + 1))
    return matrix, 2.0 + 2.0 * np.cos(np.pi * index / (size + 1))

def halves_of(matrix):
    high = matrix.astype(jnp.bfloat16)
    return high, (matrix - high.astype(np.float64)).astype(jnp.bfloat16)

def split(values):
    high = values.astype(jnp.bfloat16)
    return high, (values - high.astype(jnp.float32)).astype(jnp.bfloat16)

def dot(a, b):
    return jnp.dot(a, b, preferred_element_type=jnp.float32)

def factors_kernel(coef_ref, left_ref, right_ref, out_ref):
    term_count, power_count = coef_ref.shape[1:]
    block = 32
    def rows_step(i, carry):
        rows = pl.ds(pl.multiple_of(i * block, block), block)
        g = left_ref[rows, :] * right_ref[0:1, :] * 0.125 - 1.0
        twice = 2.0 * g
        sums = [[coef_ref[c, 0, j] + coef_ref[c, 1, j] * g for c in range(2)] for j in range(power_count)]
        before, now = jnp.ones_like(g), g
        for k in range(2, term_count):
            before, now = now, twice * now - before
            for j in range(power_count):
                for c in range(2):
                    sums[j][c] = sums[j][c] + coef_ref[c, k, j] * now
        for j in range(power_count):
            for c in range(2):
                out_ref[j, c, rows, :] = sums[j][c]
        return carry
    lax.fori_loop(0, left_ref.shape[0] // block, rows_step, 0)

def spectral_factors(poly_coef, nx, ny):
    _, lx = sine_transform(nx)
    _, ly = sine_transform(ny)
    left = jnp.asarray(np.broadcast_to(lx[:, None], (nx, 1)), jnp.float32)
    right = jnp.asarray(ly[None, :], jnp.float32)
    vmem = pl.BlockSpec(memory_space=pltpu.VMEM)
    return pl.pallas_call(
        factors_kernel,
        out_shape=jax.ShapeDtypeStruct((poly_coef.shape[2], 2, nx, ny), jnp.float32),
        in_specs=[pl.BlockSpec(memory_space=pltpu.SMEM), vmem, vmem],
        out_specs=vmem,
        compiler_params=pltpu.CompilerParams(vmem_limit_bytes=16 * 1024 * 1024),
        cost_estimate=pl.CostEstimate(
            flops=poly_coef.size * 2 * nx * ny, bytes_accessed=32 * nx * ny, transcendentals=0
        ),
        name="spectral_factors",
    )(poly_coef, left, right)

def depth_kernel(scale_ref, core_ref, left_ref, right_ref, factor_ref, start_ref, mine_ref, other_ref,
                 image_ref, field_ref, state, spectrum, *, image_scale):
    depth_count = image_ref.shape[0]
    power_count, _, nx, ny = factor_ref.shape
    held = mine_ref.shape[0]
    state[...] = start_ref[...]

    def along_y(values):
        high, low = split(values)
        return dot(jnp.concatenate([high, low, high], axis=1), right_ref[...])

    def along_x(values):
        high, low = split(values)
        return dot(left_ref[...], jnp.concatenate([high, high, low], axis=0))

    def depth_step(z, carry):
        for c in range(2):
            spectrum[c] = along_x(along_y(state[c]))

        def finish(ref):
            slow = scale_ref[0] / ref[z % held]
            for c in range(2):
                total = None
                for j in range(power_count - 1, -1, -1):
                    if c == 0:
                        part = factor_ref[j, 0] * spectrum[0] - factor_ref[j, 1] * spectrum[1]
                    else:
                        part = factor_ref[j, 0] * spectrum[1] + factor_ref[j, 1] * spectrum[0]
                    part = along_y(along_x(part))
                    total = part if total is None else total * slow + part
                state[c] = total

        @pl.when(z // held == core_ref[0])
        def _():
            finish(mine_ref)

        @pl.when(z // held != core_ref[0])
        def _():
            finish(other_ref)

        image_ref[z] = state[0] * image_scale
        return carry

    lax.fori_loop(0, depth_count, depth_step, 0)
    field_ref[...] = state[...]

def depth_steps(scale, core, factors, start, mine, other, depth_count, image_scale):
    _, nx, ny = start.shape
    sx, _ = sine_transform(nx)
    sy, _ = sine_transform(ny)
    xh, xl = halves_of(sx)
    yh, yl = halves_of(sy)
    left = jnp.asarray(np.concatenate([xh, xl, xh], axis=1))
    right = jnp.asarray(np.concatenate([yh, yh, yl], axis=0))
    def kernel(*refs):
        depth_kernel(*refs, image_scale=image_scale)
    smem = pl.BlockSpec(memory_space=pltpu.SMEM)
    vmem = pl.BlockSpec(memory_space=pltpu.VMEM)
    return pl.pallas_call(
        kernel,
        out_shape=(jax.ShapeDtypeStruct((depth_count, nx, ny), jnp.float32),
                   jax.ShapeDtypeStruct((2, nx, ny), jnp.float32)),
        in_specs=[smem, smem] + [vmem] * 6,
        out_specs=(vmem, vmem),
        scratch_shapes=[pltpu.VMEM((2, nx, ny), jnp.float32), pltpu.VMEM((2, nx, ny), jnp.float32)],
        compiler_params=pltpu.CompilerParams(vmem_limit_bytes=32 * 1024 * 1024),
        cost_estimate=pl.CostEstimate(
            flops=depth_count * 120 * nx * ny * (nx + ny) // 2, bytes_accessed=64 * nx * ny, transcendentals=0
        ),
        name="depth_steps",
    )(scale, core, left, right, factors, start, mine, other)


def swap_cores(array, count):
    return lax.ppermute(array, "freq", [(i, i ^ 1) for i in range(count)])


def on_device(traces, velocity, poly_coef, freq_slot, depth_owner):
    devices = lax.axis_size("freq")
    total_freq = freq_slot.shape[0]
    local_x, ny, sample_count = traces.shape
    nx = devices * local_x
    depth_count = depth_owner.shape[0]
    me = lax.axis_index("freq")
    core = me % 2

    by_rows = lax.all_to_all(
        velocity.reshape(devices, local_x, ny), "freq", split_axis=0, concat_axis=0, tiled=True
    )
    chosen = jnp.stack(
        [lax.dynamic_index_in_dim(by_rows, depth_owner[z], 0, keepdims=False) for z in range(depth_count)]
    ).astype(jnp.float16)

    freq_bin = freq_slot + 1
    sample_index = jnp.arange(sample_count, dtype=jnp.int32)
    phase_int = freq_bin[:, None] * sample_index[None, :] % sample_count
    phases = phase_int.astype(jnp.float32) * (2.0 * math.pi / sample_count)
    dft_table = (jnp.stack([jnp.cos(phases), -jnp.sin(phases)]) / math.sqrt(sample_count)).astype(
        jnp.bfloat16
    )
    spectra = jnp.einsum("cft,xyt->fcxy", dft_table, traces, preferred_element_type=jnp.float32)
    spectra = (spectra * 512.0).astype(jnp.float16)

    held = depth_count // 2
    halves = jnp.broadcast_to(
        chosen.reshape(1, 2, held, local_x, ny), (devices // 2, 2, held, local_x, ny)
    ).reshape(devices, held, local_x, ny)
    received = lax.all_to_all(
        jnp.concatenate([spectra, halves], axis=1), "freq", split_axis=0, concat_axis=0, tiled=True
    )
    gathered = received.transpose(1, 0, 2, 3).reshape(2 + held, nx, ny)
    start = gathered[:2].astype(jnp.float32) * (1.0 / 512.0)
    mine_half = gathered[2:]
    other_half = swap_cores(mine_half, devices)
    mine, other = mine_half.astype(jnp.float32), other_half.astype(jnp.float32)

    freq_value = lax.dynamic_index_in_dim(freq_bin, me, 0, keepdims=False).astype(jnp.float32)
    images, wavefield = depth_steps(
        (freq_value / total_freq).reshape(1),
        core.astype(jnp.int32).reshape(1),
        spectral_factors(poly_coef, nx, ny),
        start,
        mine,
        other,
        depth_count,
        1.0 / math.sqrt(total_freq),
    )

    by_core = images.reshape(depth_count, devices // 2, 2, local_x, ny)
    keep = lax.dynamic_index_in_dim(by_core, core, 2, keepdims=False)
    send = lax.dynamic_index_in_dim(by_core, 1 - core, 2, keepdims=False)
    pair_sum = keep + swap_cores(send, devices)
    same_core = [[i for i in range(devices) if i % 2 == c] for c in range(2)]
    shares = lax.all_to_all(
        pair_sum.transpose(1, 0, 2, 3),
        "freq",
        split_axis=0,
        concat_axis=0,
        tiled=True,
        axis_index_groups=same_core,
    )
    return (jnp.sum(shares, axis=0), wavefield[:, None])


def solution(mesh):
    return jax.shard_map(
        on_device,
        mesh=mesh,
        in_specs=(
            P(("group", "freq"), None, None),
            P(("group", "freq"), None, None),
            P(),
            P(),
            P("group"),
        ),
        out_specs=(P(None, ("group", "freq"), None), P(None, ("group", "freq"), None, None)),
        check_vma=False,
    )
```

```python
import math

import jax
import jax.numpy as jnp
import numpy as np
from jax import lax
from jax.experimental import pallas as pl
from jax.experimental.pallas import tpu as pltpu
from jax.sharding import PartitionSpec as P

SPECTRA_SCALE = 512.0


def sine_transform(size):
    index = np.arange(1, size + 1)
    matrix = np.sqrt(2.0 / (size + 1)) * np.sin(np.pi * np.outer(index, index) / (size + 1))
    return matrix, 2.0 + 2.0 * np.cos(np.pi * index / (size + 1))

def halves_of(matrix):
    high = matrix.astype(jnp.bfloat16)
    return high, (matrix - high.astype(np.float64)).astype(jnp.bfloat16)

def split(values):
    high = values.astype(jnp.bfloat16)
    return high, (values - high.astype(jnp.float32)).astype(jnp.bfloat16)

def dot(a, b):
    return jnp.dot(a, b, preferred_element_type=jnp.float32)

def factors_kernel(coef_ref, left_ref, right_ref, out_ref):
    term_count, power_count = coef_ref.shape[1:]
    block = 32
    def rows_step(i, carry):
        rows = pl.ds(pl.multiple_of(i * block, block), block)
        g = left_ref[rows, :] * right_ref[0:1, :] * 0.125 - 1.0
        twice = 2.0 * g
        sums = [[coef_ref[c, 0, j] + coef_ref[c, 1, j] * g for c in range(2)] for j in range(power_count)]
        before, now = jnp.ones_like(g), g
        for k in range(2, term_count):
            before, now = now, twice * now - before
            for j in range(power_count):
                for c in range(2):
                    sums[j][c] = sums[j][c] + coef_ref[c, k, j] * now
        for j in range(power_count):
            for c in range(2):
                out_ref[j, c, rows, :] = sums[j][c]
        return carry
    lax.fori_loop(0, left_ref.shape[0] // block, rows_step, 0)

def spectral_factors(poly_coef, nx, ny):
    _, lx = sine_transform(nx)
    _, ly = sine_transform(ny)
    left = jnp.asarray(np.broadcast_to(lx[:, None], (nx, 1)), jnp.float32)
    right = jnp.asarray(ly[None, :], jnp.float32)
    vmem = pl.BlockSpec(memory_space=pltpu.VMEM)
    return pl.pallas_call(
        factors_kernel,
        out_shape=pltpu.HBM((poly_coef.shape[2], 2, nx, ny), jnp.float32),
        in_specs=[pl.BlockSpec(memory_space=pltpu.SMEM), vmem, vmem],
        out_specs=vmem,
        compiler_params=pltpu.CompilerParams(vmem_limit_bytes=6 * 1024 * 1024),
        cost_estimate=pl.CostEstimate(
            flops=poly_coef.size * 2 * nx * ny, bytes_accessed=32 * nx * ny, transcendentals=0
        ),
        name="spectral_factors",
    )(poly_coef, left, right)

def right_product(values, matrix_ref):
    high, low = split(values)
    return dot(high, matrix_ref[0]) + dot(low, matrix_ref[0]) + dot(high, matrix_ref[1])


def left_product(matrix_ref, values):
    high, low = split(values)
    return dot(matrix_ref[0], high) + dot(matrix_ref[0], low) + dot(matrix_ref[1], high)


def step_part(left_ref, right_ref, factor_ref, spectrum, j, c):
    if c == 0:
        mixed = factor_ref[j, 0] * spectrum[0] - factor_ref[j, 1] * spectrum[1]
    else:
        mixed = factor_ref[j, 0] * spectrum[1] + factor_ref[j, 1] * spectrum[0]
    return right_product(left_product(left_ref, mixed), right_ref)


def first_kernel(left_ref, right_ref, factor_hbm, start_ref, part_ref, spectrum, factor_ref, sem):
    fetch = pltpu.make_async_copy(factor_hbm, factor_ref, sem)
    fetch.start()
    for c in range(2):
        spectrum[c] = left_product(left_ref, right_product(start_ref[c], right_ref))
    fetch.wait()
    for j in range(part_ref.shape[0]):
        for c in range(2):
            part_ref[j, c] = step_part(left_ref, right_ref, factor_ref, spectrum, j, c)


def depth_kernel(
    slot_ref, place_ref, left_ref, right_ref, factor_hbm, part_ref, mine_ref, other_ref,
    keep_ref, send_ref, field_ref, state, spectrum, slow, factor_ref, sems, *, total_freq,
):
    chips, depth_count, local_x, _ = mine_ref.shape
    power_count = factor_ref.shape[0]
    image_scale = 1.0 / math.sqrt(total_freq)
    scale = (slot_ref[place_ref[0]] + 1).astype(jnp.float32) / total_freq
    core = lax.rem(place_ref[0], 2)

    def rows_of(chip, number):
        first = (2 * chip + number) * local_x
        return slice(first, first + local_x)

    def load_slow(z):
        for number in range(2):
            @pl.when(core == number)
            def _():
                for chip in range(chips):
                    slow[rows_of(chip, number), :] = scale / mine_ref[chip, z].astype(jnp.float32)
                    slow[rows_of(chip, 1 - number), :] = scale / other_ref[chip, z].astype(jnp.float32)

    def store_image(z):
        for number in range(2):
            @pl.when(core == number)
            def _():
                for chip in range(chips):
                    keep_ref[chip, z] = state[0, rows_of(chip, number), :] * image_scale
                    send_ref[chip, z] = state[0, rows_of(chip, 1 - number), :] * image_scale

    fetches = [
        pltpu.make_async_copy(factor_hbm.at[j], factor_ref.at[j], sems.at[j]) for j in range(power_count)
    ]
    for fetch in fetches:
        fetch.start()
    load_slow(0)
    for c in range(2):
        total = part_ref[power_count - 1, c]
        for j in range(power_count - 2, -1, -1):
            total = total * slow[...] + part_ref[j, c]
        state[c] = total
    store_image(0)

    def depth_step(z, carry):
        load_slow(z)
        for c in range(2):
            spectrum[c] = left_product(left_ref, right_product(state[c], right_ref))

        @pl.when(z == 1)
        def _():
            for fetch in fetches:
                fetch.wait()

        for c in range(2):
            state[c] = step_part(left_ref, right_ref, factor_ref, spectrum, power_count - 1, c)
            for j in range(power_count - 2, -1, -1):
                state[c] = state[c] * slow[...] + step_part(left_ref, right_ref, factor_ref, spectrum, j, c)
        store_image(z)
        return carry

    lax.fori_loop(1, depth_count, depth_step, 0)
    field_ref[...] = state[...]
    peak = jnp.max(jnp.abs(keep_ref[:, :depth_count]), axis=(0, 1))
    peak = jnp.maximum(peak, jnp.max(jnp.abs(send_ref[:, :depth_count]), axis=(0, 1)))
    peak = jnp.max(jnp.max(peak, axis=0, keepdims=True), axis=1, keepdims=True)
    for chip in range(chips):
        keep_ref[chip, depth_count] = jnp.broadcast_to(peak, keep_ref.shape[2:])
        send_ref[chip, depth_count] = jnp.broadcast_to(peak, keep_ref.shape[2:])


def transform(size):
    return jnp.asarray(np.stack(halves_of(sine_transform(size)[0])))


SMEM = pl.BlockSpec(memory_space=pltpu.SMEM)
VMEM = pl.BlockSpec(memory_space=pltpu.VMEM)
HBM = pl.BlockSpec(memory_space=pltpu.HBM)


def in_vmem(array):
    return pltpu.with_memory_space_constraint(array, pltpu.VMEM)


def in_hbm(array):
    return pltpu.with_memory_space_constraint(array, pltpu.HBM)


def first_parts(left, right, factors, start):
    power_count, _, nx, ny = factors.shape
    return pl.pallas_call(
        first_kernel,
        out_shape=pltpu.VMEM((power_count, 2, nx, ny), jnp.float32),
        in_specs=[VMEM, VMEM, HBM, VMEM],
        out_specs=VMEM,
        scratch_shapes=[
            pltpu.VMEM((2, nx, ny), jnp.float32),
            pltpu.VMEM(factors.shape, jnp.float32),
            pltpu.SemaphoreType.DMA,
        ],
        compiler_params=pltpu.CompilerParams(vmem_limit_bytes=8 * 1024 * 1024),
        cost_estimate=pl.CostEstimate(
            flops=120 * nx * ny * (nx + ny) // 2, bytes_accessed=64 * nx * ny, transcendentals=0
        ),
        name="first_parts",
    )(left, right, in_hbm(factors), start)


def depth_steps(freq_slot, place, left, right, factors, parts, mine, other):
    chips, depth_count, local_x, ny = mine.shape
    _, _, nx, _ = factors.shape

    def kernel(*refs):
        depth_kernel(*refs, total_freq=freq_slot.shape[0])

    share = jax.ShapeDtypeStruct((chips, depth_count + 1, local_x, ny), jnp.float32)
    return pl.pallas_call(
        kernel,
        out_shape=(share, share, jax.ShapeDtypeStruct((2, nx, ny), jnp.float32)),
        in_specs=[SMEM, SMEM, VMEM, VMEM, HBM, VMEM, VMEM, VMEM],
        out_specs=(VMEM, VMEM, VMEM),
        scratch_shapes=[
            pltpu.VMEM((2, nx, ny), jnp.float32),
            pltpu.VMEM((2, nx, ny), jnp.float32),
            pltpu.VMEM((nx, ny), jnp.float32),
            pltpu.VMEM(factors.shape, jnp.float32),
            pltpu.SemaphoreType.DMA((factors.shape[0],)),
        ],
        compiler_params=pltpu.CompilerParams(vmem_limit_bytes=10 * 1024 * 1024),
        cost_estimate=pl.CostEstimate(
            flops=depth_count * 120 * nx * ny * (nx + ny) // 2, bytes_accessed=64 * nx * ny, transcendentals=0
        ),
        name="depth_steps",
    )(freq_slot, place, left, right, in_hbm(factors), in_vmem(parts), mine, other)


def spectra_kernel(
    slot_hbm, table_hbm, traces_hbm, speed_hbm, out_ref, slot_ref, table_ref, traces_ref, speed_ref, bins, sems
):
    slots, _, local_x, ny = out_ref.shape
    chunk = max(local_x // 4, 1)
    copies = [
        pltpu.make_async_copy(table_hbm, table_ref, sems.at[0]),
        pltpu.make_async_copy(slot_hbm, slot_ref, sems.at[1]),
        pltpu.make_async_copy(speed_hbm, speed_ref, sems.at[2]),
    ]
    for i, x in enumerate(range(0, local_x, chunk)):
        part = pl.ds(x, chunk)
        copies.append(pltpu.make_async_copy(traces_hbm.at[part], traces_ref.at[part], sems.at[3 + i]))
    for copy in copies:
        copy.start()
    copies[0].wait()
    for i, x in enumerate(range(0, local_x, chunk)):
        copies[3 + i].wait()
        rows = traces_ref[x : x + chunk].reshape(chunk * ny, traces_ref.shape[2])
        result = lax.dot_general(
            table_ref[...], rows, (((1,), (1,)), ((), ())), preferred_element_type=jnp.float32
        )
        for k in range(chunk):
            bins[:, x + k, :] = result[:, k * ny : (k + 1) * ny]
    copies[1].wait()
    copies[2].wait()
    for f in range(slots):
        for c in range(2):
            out_ref[f, c] = bins[2 * slot_ref[f] + c] * SPECTRA_SCALE
        out_ref[f, 2] = speed_ref[f].astype(jnp.float32)


def position_spectra(freq_slot, traces, speed):
    local_x, ny, sample_count = traces.shape
    slots = freq_slot.shape[0]
    index = np.arange(1, slots + 1)[:, None] * np.arange(sample_count)[None, :] % sample_count
    phases = index.astype(np.float32) * np.float32(2.0 * math.pi / sample_count)
    table = np.stack([np.cos(phases), -np.sin(phases)], axis=1) / np.float32(math.sqrt(sample_count))
    table = jnp.asarray(table.reshape(2 * slots, sample_count).astype(jnp.bfloat16))
    return pl.pallas_call(
        spectra_kernel,
        out_shape=jax.ShapeDtypeStruct((slots, 3, local_x, ny), jnp.float32),
        in_specs=[HBM] * 4,
        out_specs=VMEM,
        scratch_shapes=[
            pltpu.SMEM((slots,), jnp.int32),
            pltpu.VMEM((2 * slots, sample_count), jnp.bfloat16),
            pltpu.VMEM(traces.shape, jnp.bfloat16),
            pltpu.VMEM(speed.shape, jnp.bfloat16),
            pltpu.VMEM((2 * slots, local_x, ny), jnp.float32),
            pltpu.SemaphoreType.DMA((7,)),
        ],
        compiler_params=pltpu.CompilerParams(vmem_limit_bytes=8 * 1024 * 1024),
        cost_estimate=pl.CostEstimate(
            flops=4 * slots * traces.size, bytes_accessed=2 * traces.size, transcendentals=0
        ),
        name="position_spectra",
    )(in_hbm(freq_slot), in_hbm(table), in_hbm(traces), in_hbm(speed))


def swap_cores(array, count):
    return lax.ppermute(array, "freq", [(i, i ^ 1) for i in range(count)])


def on_device(traces, velocity, poly_coef, freq_slot, depth_owner):
    devices = lax.axis_size("freq")
    local_x, ny, _ = traces.shape
    nx = devices * local_x
    chips = devices // 2
    depth_count = depth_owner.shape[0]
    place = lax.axis_index("freq").astype(jnp.int32).reshape(1)
    same_core = [[i for i in range(devices) if i % 2 == c] for c in range(2)]

    spectra = position_spectra(freq_slot, traces, velocity.reshape(devices, local_x, ny))
    received = lax.all_to_all(
        spectra.astype(jnp.float16), "freq", split_axis=0, concat_axis=0, tiled=True
    )
    received, factors = lax.optimization_barrier((received, spectral_factors(poly_coef, nx, ny)))
    start = received[:, :2].transpose(1, 0, 2, 3).reshape(2, nx, ny).astype(jnp.float32) / SPECTRA_SCALE

    owned = (depth_owner[:, None] == jnp.arange(devices, dtype=jnp.int32)[None, :]).astype(jnp.bfloat16)
    by_rows = received[:, 2].astype(jnp.bfloat16).reshape(devices, local_x * ny)
    chosen = jnp.dot(owned, by_rows, preferred_element_type=jnp.float32).astype(jnp.bfloat16)
    chosen = jnp.broadcast_to(
        chosen.reshape(1, depth_count, local_x, ny), (chips, depth_count, local_x, ny)
    )
    mine = lax.all_to_all(
        chosen, "freq", split_axis=0, concat_axis=0, tiled=True, axis_index_groups=same_core
    )
    left, right = transform(nx), transform(ny)
    parts, mine = lax.optimization_barrier((first_parts(left, right, factors, start), mine))
    other = swap_cores(mine, devices)
    keep, send, wavefield = depth_steps(
        freq_slot,
        place,
        left,
        right,
        factors,
        parts,
        mine,
        other,
    )

    total = keep + swap_cores(send, devices)
    power = jnp.ceil(jnp.log2(jnp.maximum(total[:, depth_count:], 1e-30)))
    packed = jnp.concatenate([total[:, :depth_count] * jnp.exp2(-power), power], axis=1)
    shares = lax.all_to_all(
        packed.astype(jnp.float16),
        "freq",
        split_axis=0,
        concat_axis=0,
        tiled=True,
        axis_index_groups=same_core,
    ).astype(jnp.float32)
    image = jnp.sum(shares[:, :depth_count] * jnp.exp2(shares[:, depth_count:]), axis=0)
    return (image, wavefield[:, None])


def solution(mesh):
    return jax.shard_map(
        on_device,
        mesh=mesh,
        in_specs=(
            P(("group", "freq"), None, None),
            P(("group", "freq"), None, None),
            P(),
            P(),
            P("group"),
        ),
        out_specs=(P(None, ("group", "freq"), None), P(None, ("group", "freq"), None, None)),
        check_vma=False,
    )
```

```python
import math

import jax
import jax.numpy as jnp
import numpy as np
from jax import lax
from jax.experimental import pallas as pl
from jax.experimental.pallas import tpu as pltpu
from jax.sharding import PartitionSpec as P

SPECTRA_SCALE = 512.0
SMEM = pl.BlockSpec(memory_space=pltpu.SMEM)
VMEM = pl.BlockSpec(memory_space=pltpu.VMEM)
HBM = pl.BlockSpec(memory_space=pltpu.HBM)


def in_vmem(array):
    return pltpu.with_memory_space_constraint(array, pltpu.VMEM)


def in_hbm(array):
    return pltpu.with_memory_space_constraint(array, pltpu.HBM)


def eigenvalues(size):
    values = 2.0 + 2.0 * np.cos(np.pi * np.arange(1, size + 1) / (size + 1))
    return np.concatenate([values[0::2], values[1::2]])


def folded_sines(size):
    index = np.arange(1, size + 1)
    matrix = np.sqrt(2.0 / (size + 1)) * np.sin(np.pi * np.outer(index, index) / (size + 1))
    return matrix[: size // 2, 0::2], matrix[: size // 2, 1::2]


def right_matrices(size):
    out = []
    even, odd = folded_sines(size)
    for matrix in (even, odd, even.T, odd.T):
        high = matrix.astype(jnp.bfloat16)
        low = (matrix - high.astype(np.float64)).astype(jnp.bfloat16)
        out.append(np.block([[high, low], [high, np.zeros_like(low)]]))
    return np.stack(out)


def fold_order(size):
    half = size // 2
    return np.concatenate([np.arange(half), np.arange(size - 1, half - 1, -1)])


def fold_matrix(size):
    return np.eye(size)[fold_order(size)].astype(jnp.bfloat16)


def split(values):
    high = values.astype(jnp.bfloat16)
    return high, (values - high.astype(jnp.float32)).astype(jnp.bfloat16)


def dot(a, b):
    return jnp.dot(a, b, preferred_element_type=jnp.float32)


def along_y(values, matrix):
    half = values.shape[1]
    both = dot(jnp.concatenate(split(values), axis=1), matrix)
    return both[:, :half] + both[:, half:]


def along_x(values, matrix):
    half = values.shape[0]
    both = dot(matrix, jnp.concatenate(split(values), axis=0))
    return both[:half] + both[half:]


def forward(values, left_ref, right_ref):
    half = values.shape[1] // 2
    a, b = values[:, :half], values[:, half:]
    values = jnp.concatenate([along_y(a + b, right_ref[0]), along_y(a - b, right_ref[1])], axis=1)
    half = values.shape[0] // 2
    a, b = values[:half], values[half:]
    return jnp.concatenate([along_x(a + b, left_ref[0]), along_x(a - b, left_ref[1])], axis=0)


def inverse_x(values, left_ref):
    half = values.shape[0] // 2
    even, odd = along_x(values[:half], left_ref[2]), along_x(values[half:], left_ref[3])
    return jnp.concatenate([even + odd, even - odd], axis=0)


def inverse_y(values, right_ref):
    half = values.shape[1] // 2
    even, odd = along_y(values[:, :half], right_ref[2]), along_y(values[:, half:], right_ref[3])
    return jnp.concatenate([even + odd, even - odd], axis=1)


def reorder(values, left, right):
    high, low = split(values)
    values = dot(high, right) + dot(low, right)
    high, low = split(values)
    return dot(left, high) + dot(left, low)


def half_parts(left_ref, factor_ref, spectrum, columns, parts):
    for j in range(factor_ref.shape[0]):
        for c in parts:
            if c == 0:
                mixed = factor_ref[j, 0] * spectrum[0] - factor_ref[j, 1] * spectrum[1]
            else:
                mixed = factor_ref[j, 0] * spectrum[1] + factor_ref[j, 1] * spectrum[0]
            columns[j, c] = inverse_x(mixed, left_ref)


def sum_powers(right_ref, columns, slow, state, parts):
    power_count = columns.shape[0]
    for j in range(power_count - 1, -1, -1):
        for c in parts:
            part = inverse_y(columns[j, c], right_ref)
            state[c] = part if j == power_count - 1 else state[c] * slow[...] + part


def factors_kernel(coef_ref, left_ref, right_ref, out_ref):
    term_count, power_count = coef_ref.shape[1:]
    block = 32

    def rows_step(i, carry):
        rows = pl.ds(pl.multiple_of(i * block, block), block)
        g = left_ref[rows, :] * right_ref[0:1, :] * 0.125 - 1.0
        twice = 2.0 * g
        sums = [[coef_ref[c, 0, j] + coef_ref[c, 1, j] * g for c in range(2)] for j in range(power_count)]
        before, now = jnp.ones_like(g), g
        for k in range(2, term_count):
            before, now = now, twice * now - before
            for j in range(power_count):
                for c in range(2):
                    sums[j][c] = sums[j][c] + coef_ref[c, k, j] * now
        for j in range(power_count):
            for c in range(2):
                out_ref[j, c, rows, :] = sums[j][c]
        return carry

    lax.fori_loop(0, left_ref.shape[0] // block, rows_step, 0)


def spectral_factors(poly_coef, nx, ny):
    return pl.pallas_call(
        factors_kernel,
        out_shape=pltpu.HBM((poly_coef.shape[2], 2, nx, ny), jnp.float32),
        in_specs=[SMEM, VMEM, VMEM],
        out_specs=VMEM,
        compiler_params=pltpu.CompilerParams(vmem_limit_bytes=6 * 1024 * 1024),
        cost_estimate=pl.CostEstimate(
            flops=poly_coef.size * 2 * nx * ny, bytes_accessed=32 * nx * ny, transcendentals=0
        ),
        name="spectral_factors",
    )(
        poly_coef,
        jnp.asarray(eigenvalues(nx)[:, None], jnp.float32),
        jnp.asarray(eigenvalues(ny)[None, :], jnp.float32),
    )


def first_kernel(
    left_ref, right_ref, order_x_ref, order_y_ref, factor_hbm, start_ref, part_ref, spectrum, columns, factor_ref, sem
):
    fetch = pltpu.make_async_copy(factor_hbm, factor_ref, sem)
    fetch.start()
    for c in range(2):
        spectrum[c] = forward(reorder(start_ref[c], order_x_ref[...], order_y_ref[...]), left_ref, right_ref)
    fetch.wait()
    half_parts(left_ref, factor_ref, spectrum, columns, range(2))
    for j in range(part_ref.shape[0]):
        for c in range(2):
            part_ref[j, c] = inverse_y(columns[j, c], right_ref)


def first_parts(left, right, order_x, order_y, factors, start):
    power_count, _, nx, ny = factors.shape
    return pl.pallas_call(
        first_kernel,
        out_shape=pltpu.VMEM((power_count, 2, nx, ny), jnp.float32),
        in_specs=[VMEM, VMEM, VMEM, VMEM, HBM, VMEM],
        out_specs=VMEM,
        scratch_shapes=[
            pltpu.VMEM((2, nx, ny), jnp.float32),
            pltpu.VMEM(factors.shape, jnp.float32),
            pltpu.VMEM(factors.shape, jnp.float32),
            pltpu.SemaphoreType.DMA,
        ],
        compiler_params=pltpu.CompilerParams(vmem_limit_bytes=10 * 1024 * 1024),
        cost_estimate=pl.CostEstimate(
            flops=80 * nx * ny * (nx + ny) // 2, bytes_accessed=64 * nx * ny, transcendentals=0
        ),
        name="first_parts",
    )(left, right, order_x, order_y, in_hbm(factors), start)


def depth_kernel(
    slot_ref, place_ref, left_hbm, right_hbm, factor_hbm, part_ref, speed_ref,
    keep_ref, send_ref, spectrum, real_ref, slow, state, columns, left_ref, right_ref, factor_ref, sems,
    *, total_freq,
):
    _, chips, depth_count, local_x, _ = speed_ref.shape
    power_count = factor_ref.shape[0]
    nx, ny = slow.shape
    image_scale = 1.0 / math.sqrt(total_freq)
    scale = (slot_ref[place_ref[0]] + 1).astype(jnp.float32) / total_freq
    core = lax.rem(place_ref[0], 2)

    def rows_of(chip, number):
        block = 2 * chip + number
        if block >= chips:
            block = 3 * chips - 1 - block
        return slice(block * local_x, (block + 1) * local_x)

    def load_slow(z):
        for number in range(2):
            @pl.when(core == number)
            def _():
                for chip in range(chips):
                    slow[rows_of(chip, number), :] = scale / speed_ref[0, chip, z].astype(jnp.float32)
                    slow[rows_of(chip, 1 - number), :] = scale / speed_ref[1, chip, z].astype(jnp.float32)

    def store_image(z):
        half = ny // 2
        for number in range(2):
            @pl.when(core == number)
            def _():
                for chip in range(chips):
                    for side in range(2):
                        lanes = slice(side * half, (side + 1) * half)
                        keep_ref[chip, 2 * z + side] = state[0, rows_of(chip, number), lanes] * image_scale
                        send_ref[chip, 2 * z + side] = state[0, rows_of(chip, 1 - number), lanes] * image_scale

    sides = [
        pltpu.make_async_copy(right_hbm, right_ref, sems.at[0]),
        pltpu.make_async_copy(left_hbm, left_ref, sems.at[1]),
    ]
    fetch = pltpu.make_async_copy(factor_hbm, factor_ref, sems.at[2])
    for copy in sides:
        copy.start()
    fetch.start()
    load_slow(0)
    for c in range(2):
        total = part_ref[power_count - 1, c]
        for j in range(power_count - 2, -1, -1):
            total = total * slow[...] + part_ref[j, c]
        state[c] = total
    store_image(0)

    for copy in sides:
        copy.wait()

    def to_spectrum(z):
        load_slow(z)
        for c in range(2):
            spectrum[c] = forward(state[c], left_ref, right_ref)

        @pl.when(z == 1)
        def _():
            fetch.wait()

    def depth_step(z, carry):
        to_spectrum(z)
        half_parts(left_ref, factor_ref, spectrum, columns, range(2))
        sum_powers(right_ref, columns, slow, state, range(2))
        store_image(z)
        return carry

    lax.fori_loop(1, depth_count - 1, depth_step, 0)
    to_spectrum(depth_count - 1)
    half_parts(left_ref, factor_ref, spectrum, columns, range(1))
    sum_powers(right_ref, columns, slow, state, range(1))
    store_image(depth_count - 1)
    real_ref[...] = state[0]
    shares = 2 * depth_count
    peak = jnp.max(jnp.abs(keep_ref[:, :shares]), axis=(0, 1))
    peak = jnp.maximum(peak, jnp.max(jnp.abs(send_ref[:, :shares]), axis=(0, 1)))
    peak = jnp.max(jnp.max(peak, axis=0, keepdims=True), axis=1, keepdims=True)
    for chip in range(chips):
        keep_ref[chip, shares] = jnp.broadcast_to(peak, keep_ref.shape[2:])
        send_ref[chip, shares] = jnp.broadcast_to(peak, keep_ref.shape[2:])


def depth_steps(freq_slot, place, left, right, factors, parts, speed):
    _, chips, depth_count, local_x, ny = speed.shape
    nx = factors.shape[2]

    def kernel(*refs):
        depth_kernel(*refs, total_freq=freq_slot.shape[0])

    share = jax.ShapeDtypeStruct((chips, 2 * depth_count + 1, local_x, ny // 2), jnp.float32)
    field = jax.ShapeDtypeStruct((nx, ny), jnp.float32)
    return pl.pallas_call(
        kernel,
        out_shape=(share, share, jax.ShapeDtypeStruct((2, nx, ny), jnp.float32), field, field),
        in_specs=[SMEM, SMEM, HBM, HBM, HBM, VMEM, VMEM],
        out_specs=(VMEM,) * 5,
        scratch_shapes=[
            pltpu.VMEM((2, nx, ny), jnp.float32),
            pltpu.VMEM(factors.shape, jnp.float32),
            pltpu.VMEM(left.shape, jnp.bfloat16),
            pltpu.VMEM(right.shape, jnp.bfloat16),
            pltpu.VMEM(factors.shape, jnp.float32),
            pltpu.SemaphoreType.DMA((3,)),
        ],
        compiler_params=pltpu.CompilerParams(vmem_limit_bytes=12 * 1024 * 1024),
        cost_estimate=pl.CostEstimate(
            flops=depth_count * 80 * nx * ny * (nx + ny) // 2, bytes_accessed=64 * nx * ny, transcendentals=0
        ),
        name="depth_steps",
    )(freq_slot, place, in_hbm(left), in_hbm(right), in_hbm(factors), in_vmem(parts), speed)


def last_kernel(
    left_hbm, right_hbm, order_x_hbm, order_y_hbm, factor_hbm, spectrum, real_ref, slow,
    field_ref, state, columns, left_ref, right_ref, order_x_ref, order_y_ref, factor_ref, sems,
):
    pairs = [
        (order_y_hbm, order_y_ref), (order_x_hbm, order_x_ref), (left_hbm, left_ref), (right_hbm, right_ref),
        (factor_hbm, factor_ref),
    ]
    copies = [pltpu.make_async_copy(source, target, sems.at[i]) for i, (source, target) in enumerate(pairs)]
    for copy in copies:
        copy.start()
    for copy in copies[:2]:
        copy.wait()
    field_ref[0] = reorder(real_ref[...], order_x_ref[...], order_y_ref[...])
    for copy in copies[2:]:
        copy.wait()
    half_parts(left_ref, factor_ref, spectrum, columns, range(1, 2))
    sum_powers(right_ref, columns, slow, state, range(1, 2))
    field_ref[1] = reorder(state[1], order_x_ref[...], order_y_ref[...])


def last_field(left, right, order_x, order_y, factors, spectrum, real, slow):
    _, nx, ny = spectrum.shape
    tables = [left, right, order_x, order_y, factors]
    return pl.pallas_call(
        last_kernel,
        out_shape=jax.ShapeDtypeStruct((2, nx, ny), jnp.float32),
        in_specs=[HBM] * 5 + [VMEM] * 3,
        out_specs=VMEM,
        scratch_shapes=[
            pltpu.VMEM((2, nx, ny), jnp.float32),
            pltpu.VMEM(factors.shape, jnp.float32),
            *(pltpu.VMEM(table.shape, table.dtype) for table in tables),
            pltpu.SemaphoreType.DMA((5,)),
        ],
        compiler_params=pltpu.CompilerParams(vmem_limit_bytes=14 * 1024 * 1024),
        cost_estimate=pl.CostEstimate(
            flops=40 * nx * ny * (nx + ny) // 2, bytes_accessed=64 * nx * ny, transcendentals=0
        ),
        name="last_field",
    )(*(in_hbm(table) for table in tables), spectrum, real, slow)


def spectra_kernel(
    slot_hbm, table_hbm, traces_hbm, speed_hbm, rows_hbm, lanes_hbm,
    out_ref, slot_ref, table_ref, traces_ref, speed_ref, rows_ref, lanes_ref, bins, sems,
):
    slots, _, local_x, ny = out_ref.shape
    chunk = max(local_x // 4, 1)
    pairs = [
        (table_hbm, table_ref), (slot_hbm, slot_ref), (speed_hbm, speed_ref), (lanes_hbm, lanes_ref),
        (rows_hbm, rows_ref),
    ]
    copies = [pltpu.make_async_copy(source, target, sems.at[i]) for i, (source, target) in enumerate(pairs)]
    small = len(copies)
    for i, x in enumerate(range(0, local_x, chunk)):
        part = pl.ds(x, chunk)
        copies.append(pltpu.make_async_copy(traces_hbm.at[part], traces_ref.at[part], sems.at[small + i]))
    for copy in copies:
        copy.start()
    for copy in copies[:small]:
        copy.wait()
    speed = dot(rows_ref[...], dot(speed_ref[...], lanes_ref[...]).astype(jnp.bfloat16))
    for f in range(slots):
        out_ref[f, 2] = speed[f * local_x : (f + 1) * local_x]
    for i, x in enumerate(range(0, local_x, chunk)):
        copies[small + i].wait()
        rows = traces_ref[x : x + chunk].reshape(chunk * ny, traces_ref.shape[2])
        result = lax.dot_general(
            table_ref[...], rows, (((1,), (1,)), ((), ())), preferred_element_type=jnp.float32
        )
        for k in range(chunk):
            bins[:, x + k, :] = result[:, k * ny : (k + 1) * ny]
    for f in range(slots):
        for c in range(2):
            out_ref[f, c] = bins[2 * slot_ref[f] + c] * SPECTRA_SCALE


def position_spectra(freq_slot, traces, speed):
    local_x, ny, sample_count = traces.shape
    slots = freq_slot.shape[0]
    nx = speed.shape[0]
    index = np.arange(1, slots + 1)[:, None] * np.arange(sample_count)[None, :] % sample_count
    phases = index.astype(np.float32) * np.float32(2.0 * math.pi / sample_count)
    table = np.stack([np.cos(phases), -np.sin(phases)], axis=1) / np.float32(math.sqrt(sample_count))
    table = jnp.asarray(table.reshape(2 * slots, sample_count).astype(jnp.bfloat16))
    order = np.arange(nx).reshape(-1, local_x)
    order[order.shape[0] // 2 :] = order[order.shape[0] // 2 :, ::-1]
    rows = jnp.asarray(np.eye(nx)[order.reshape(-1)].astype(jnp.bfloat16))
    lanes = jnp.asarray(fold_matrix(ny))
    chunk = max(local_x // 4, 1)
    return pl.pallas_call(
        spectra_kernel,
        out_shape=jax.ShapeDtypeStruct((slots, 3, local_x, ny), jnp.float32),
        in_specs=[HBM] * 6,
        out_specs=VMEM,
        scratch_shapes=[
            pltpu.SMEM((slots,), jnp.int32),
            pltpu.VMEM((2 * slots, sample_count), jnp.bfloat16),
            pltpu.VMEM(traces.shape, jnp.bfloat16),
            pltpu.VMEM(speed.shape, jnp.bfloat16),
            pltpu.VMEM((nx, nx), jnp.bfloat16),
            pltpu.VMEM((ny, ny), jnp.bfloat16),
            pltpu.VMEM((2 * slots, local_x, ny), jnp.float32),
            pltpu.SemaphoreType.DMA((5 + local_x // chunk,)),
        ],
        compiler_params=pltpu.CompilerParams(vmem_limit_bytes=8 * 1024 * 1024),
        cost_estimate=pl.CostEstimate(
            flops=4 * slots * traces.size, bytes_accessed=2 * traces.size, transcendentals=0
        ),
        name="position_spectra",
    )(in_hbm(freq_slot), in_hbm(table), in_hbm(traces), in_hbm(speed), in_hbm(rows), in_hbm(lanes))


def exact_dot(a, b):
    return jnp.dot(a, b, preferred_element_type=jnp.float32, precision=lax.Precision.HIGHEST)


def image_kernel(place_ref, lanes_ref, rows_ref, share_ref, image_ref):
    depth_count, local_x, ny = image_ref.shape
    half = ny // 2
    total = jnp.sum(share_ref[:, : 2 * depth_count] * jnp.exp2(share_ref[:, 2 * depth_count :]), axis=0)
    turned = exact_dot(
        jnp.concatenate([total[2 * z + 1] for z in range(depth_count)], axis=0), lanes_ref[...]
    )
    image = jnp.concatenate(
        [jnp.concatenate([total[2 * z] for z in range(depth_count)], axis=0), turned], axis=1
    )
    upper = place_ref[0] >= share_ref.shape[0]

    @pl.when(upper)
    def _():
        image_ref[...] = exact_dot(rows_ref[...], image).reshape(image_ref.shape)

    @pl.when(jnp.logical_not(upper))
    def _():
        image_ref[...] = image.reshape(image_ref.shape)


def image_rows(place, shares):
    _, parts, local_x, half = shares.shape
    depth_count = parts // 2
    lanes = jnp.asarray(np.eye(half)[::-1], jnp.float32)
    rows = jnp.asarray(np.kron(np.eye(depth_count), np.eye(local_x)[::-1]), jnp.float32)
    return pl.pallas_call(
        image_kernel,
        out_shape=jax.ShapeDtypeStruct((depth_count, local_x, 2 * half), jnp.float32),
        in_specs=[SMEM, VMEM, VMEM, VMEM],
        out_specs=VMEM,
        compiler_params=pltpu.CompilerParams(vmem_limit_bytes=4 * 1024 * 1024),
        name="image_rows",
    )(place, lanes, rows, shares)


def swap_cores(array, count):
    return lax.ppermute(array, "freq", [(i, i ^ 1) for i in range(count)])


def on_device(traces, velocity, poly_coef, freq_slot, depth_owner):
    devices = lax.axis_size("freq")
    local_x, ny, _ = traces.shape
    nx = devices * local_x
    chips = devices // 2
    depth_count = depth_owner.shape[0]
    place = lax.axis_index("freq").astype(jnp.int32).reshape(1)
    same_core = [[i for i in range(devices) if i % 2 == c] for c in range(2)]

    spectra = position_spectra(freq_slot, traces, velocity.reshape(nx, ny))
    received = lax.all_to_all(
        spectra.astype(jnp.float16), "freq", split_axis=0, concat_axis=0, tiled=True
    )
    received, factors = lax.optimization_barrier((received, spectral_factors(poly_coef, nx, ny)))
    start = received[:, :2].transpose(1, 0, 2, 3).reshape(2, nx, ny).astype(jnp.float32) / SPECTRA_SCALE

    owned = (depth_owner[:, None] == jnp.arange(devices, dtype=jnp.int32)[None, :]).astype(jnp.bfloat16)
    by_rows = received[:, 2].astype(jnp.bfloat16).reshape(devices, local_x * ny)
    chosen = jnp.dot(owned, by_rows, preferred_element_type=jnp.float32).astype(jnp.bfloat16)
    chosen = jnp.broadcast_to(
        chosen.reshape(1, depth_count, local_x, ny), (chips, depth_count, local_x, ny)
    )
    mine = lax.all_to_all(
        chosen, "freq", split_axis=0, concat_axis=0, tiled=True, axis_index_groups=same_core
    )
    left = jnp.asarray(np.swapaxes(right_matrices(nx), 1, 2))
    right = jnp.asarray(right_matrices(ny))
    order_x, order_y = jnp.asarray(fold_matrix(nx)), jnp.asarray(fold_matrix(ny))
    parts = first_parts(left, right, order_x, order_y, factors, start)
    parts, mine = lax.optimization_barrier((parts, mine))
    speed = jnp.stack([mine, swap_cores(mine, devices)])
    keep, send, spectrum, real, slow = depth_steps(
        freq_slot, place, left, right, factors, parts, speed
    )

    total = keep + swap_cores(send, devices)
    power = jnp.ceil(jnp.log2(jnp.maximum(total[:, 2 * depth_count :], 1e-30)))
    packed = jnp.concatenate([total[:, : 2 * depth_count] * jnp.exp2(-power), power], axis=1)
    shares = lax.all_to_all(
        packed.astype(jnp.float16),
        "freq",
        split_axis=0,
        concat_axis=0,
        tiled=True,
        axis_index_groups=same_core,
    )
    wavefield = last_field(left, right, order_x, order_y, factors, spectrum, real, slow)
    shares, wavefield = lax.optimization_barrier((shares, wavefield))
    return (image_rows(place, shares.astype(jnp.float32)), wavefield[:, None])


def solution(mesh):
    return jax.shard_map(
        on_device,
        mesh=mesh,
        in_specs=(
            P(("group", "freq"), None, None),
            P(("group", "freq"), None, None),
            P(),
            P(),
            P("group"),
        ),
        out_specs=(P(None, ("group", "freq"), None), P(None, ("group", "freq"), None, None)),
        check_vma=False,
    )
```

```python
import functools
import math

import jax
import jax.numpy as jnp
import numpy as np
from jax import lax
from jax.experimental import pallas as pl
from jax.experimental.pallas import tpu as pltpu
from jax.sharding import PartitionSpec as P

SPECTRA_SCALE = 512.0
SUBLANES = 8
CHUNK = 128
SMEM = pl.BlockSpec(memory_space=pltpu.SMEM)
VMEM = pl.BlockSpec(memory_space=pltpu.VMEM)
HBM = pl.BlockSpec(memory_space=pltpu.HBM)


def device_order(devices):
    length = devices // 4
    along = list(range(length // 2, -1, -1)) + list(range(length // 2 + 1, length))
    return [4 * z + 2 * y + core for y in (1, 0) for z in along for core in (1, 0)]


def chip_order(chips):
    length = chips // 2
    along = list(range(length // 2, length)) + list(range(length // 2 - 1, -1, -1))
    return [2 * z + y for y in (0, 1) for z in along]


def in_vmem(array):
    return pltpu.with_memory_space_constraint(array, pltpu.VMEM)


def in_hbm(array):
    return pltpu.with_memory_space_constraint(array, pltpu.HBM)


def eigenvalues(size):
    values = 2.0 + 2.0 * np.cos(np.pi * np.arange(1, size + 1) / (size + 1))
    return np.concatenate([values[0::2], values[1::2]])


def folded_sines(size):
    index = np.arange(1, size + 1)
    matrix = np.sqrt(2.0 / (size + 1)) * np.sin(np.pi * np.outer(index, index) / (size + 1))
    return matrix[: size // 2, 0::2], matrix[: size // 2, 1::2]


def right_matrices(size):
    out = []
    even, odd = folded_sines(size)
    for matrix in (even, odd, even.T, odd.T):
        high = matrix.astype(jnp.bfloat16)
        low = (matrix - high.astype(np.float64)).astype(jnp.bfloat16)
        out.append(np.block([[high, low], [high, np.zeros_like(low)]]))
    return np.stack(out)


def fold_order(size):
    half = size // 2
    return np.concatenate([np.arange(half), np.arange(size - 1, half - 1, -1)])


def fold_matrix(size):
    return np.eye(size)[fold_order(size)].astype(jnp.bfloat16)


def split(values):
    high = values.astype(jnp.bfloat16)
    return high, (values - high.astype(jnp.float32)).astype(jnp.bfloat16)


def dot(a, b):
    return jnp.dot(a, b, preferred_element_type=jnp.float32)


def along_y(values, matrix):
    half = values.shape[1]
    both = dot(jnp.concatenate(split(values), axis=1), matrix)
    return both[:, :half] + both[:, half:]


def along_x(values, matrix):
    half = values.shape[0]
    both = dot(matrix, jnp.concatenate(split(values), axis=0))
    return both[:half] + both[half:]


def forward(values, left_ref, right_ref):
    half = values.shape[1] // 2
    a, b = values[:, :half], values[:, half:]
    values = jnp.concatenate([along_y(a + b, right_ref[0]), along_y(a - b, right_ref[1])], axis=1)
    half = values.shape[0] // 2
    a, b = values[:half], values[half:]
    return jnp.concatenate([along_x(a + b, left_ref[0]), along_x(a - b, left_ref[1])], axis=0)


def inverse_x(values, left_ref):
    half = values.shape[0] // 2
    even, odd = along_x(values[:half], left_ref[2]), along_x(values[half:], left_ref[3])
    return jnp.concatenate([even + odd, even - odd], axis=0)


def inverse_y(values, right_ref):
    half = values.shape[1] // 2
    even, odd = along_y(values[:, :half], right_ref[2]), along_y(values[:, half:], right_ref[3])
    return jnp.concatenate([even + odd, even - odd], axis=1)


def reorder(values, left, right):
    high, low = split(values)
    values = dot(high, right) + dot(low, right)
    high, low = split(values)
    return dot(left, high) + dot(left, low)


def half_parts(left_ref, factor_ref, spectrum, columns, parts):
    for j in range(factor_ref.shape[0]):
        for c in parts:
            if c == 0:
                mixed = factor_ref[j, 0] * spectrum[0] - factor_ref[j, 1] * spectrum[1]
            else:
                mixed = factor_ref[j, 0] * spectrum[1] + factor_ref[j, 1] * spectrum[0]
            columns[j, c] = inverse_x(mixed, left_ref)


def sum_powers(right_ref, columns, slow, state, parts, chunk):
    power_count, _, nx, ny = columns.shape
    half = ny // 2
    for c in parts:
        for first in range(0, nx, chunk):
            rows = slice(first, first + chunk)
            stacked = jnp.concatenate([columns[j, c, rows, :] for j in range(power_count)], axis=0)
            even, odd = along_y(stacked[:, :half], right_ref[2]), along_y(stacked[:, half:], right_ref[3])
            low, high = even + odd, even - odd
            for values, lanes in ((low, slice(0, half)), (high, slice(half, ny))):
                total = values[(power_count - 1) * chunk :]
                for j in range(power_count - 2, -1, -1):
                    total = total * slow[rows, lanes] + values[j * chunk : (j + 1) * chunk]
                state[c, rows, lanes] = total


def factors_kernel(coef_ref, left_ref, right_ref, out_ref):
    term_count, power_count = coef_ref.shape[1:]
    block = 32

    def rows_step(i, carry):
        rows = pl.ds(pl.multiple_of(i * block, block), block)
        g = left_ref[rows, :] * right_ref[0:1, :] * 0.125 - 1.0
        twice = 2.0 * g
        sums = [[coef_ref[c, 0, j] + coef_ref[c, 1, j] * g for c in range(2)] for j in range(power_count)]
        before, now = jnp.ones_like(g), g
        for k in range(2, term_count):
            before, now = now, twice * now - before
            for j in range(power_count):
                for c in range(2):
                    sums[j][c] = sums[j][c] + coef_ref[c, k, j] * now
        for j in range(power_count):
            for c in range(2):
                out_ref[j, c, rows, :] = sums[j][c]
        return carry

    lax.fori_loop(0, left_ref.shape[0] // block, rows_step, 0)


def spectral_factors(poly_coef, nx, ny):
    return pl.pallas_call(
        factors_kernel,
        out_shape=pltpu.HBM((poly_coef.shape[2], 2, nx, ny), jnp.float32),
        in_specs=[SMEM, VMEM, VMEM],
        out_specs=VMEM,
        compiler_params=pltpu.CompilerParams(vmem_limit_bytes=6 * 1024 * 1024),
        cost_estimate=pl.CostEstimate(
            flops=poly_coef.size * 2 * nx * ny, bytes_accessed=32 * nx * ny, transcendentals=0
        ),
        name="spectral_factors",
    )(
        poly_coef,
        jnp.asarray(eigenvalues(nx)[:, None], jnp.float32),
        jnp.asarray(eigenvalues(ny)[None, :], jnp.float32),
    )


def first_kernel(
    left_ref, right_ref, order_x_ref, order_y_ref, factor_hbm, start_ref, part_ref, spectrum, columns, factor_ref, sem
):
    fetch = pltpu.make_async_copy(factor_hbm, factor_ref, sem)
    fetch.start()
    for c in range(2):
        spectrum[c] = forward(reorder(start_ref[c], order_x_ref[...], order_y_ref[...]), left_ref, right_ref)
    fetch.wait()
    half_parts(left_ref, factor_ref, spectrum, columns, range(2))
    for j in range(part_ref.shape[0]):
        for c in range(2):
            part_ref[j, c] = inverse_y(columns[j, c], right_ref)


def first_parts(left, right, order_x, order_y, factors, start):
    power_count, _, nx, ny = factors.shape
    return pl.pallas_call(
        first_kernel,
        out_shape=pltpu.VMEM((power_count, 2, nx, ny), jnp.float32),
        in_specs=[VMEM, VMEM, VMEM, VMEM, HBM, VMEM],
        out_specs=VMEM,
        scratch_shapes=[
            pltpu.VMEM((2, nx, ny), jnp.float32),
            pltpu.VMEM(factors.shape, jnp.float32),
            pltpu.VMEM(factors.shape, jnp.float32),
            pltpu.SemaphoreType.DMA,
        ],
        compiler_params=pltpu.CompilerParams(vmem_limit_bytes=10 * 1024 * 1024),
        cost_estimate=pl.CostEstimate(
            flops=80 * nx * ny * (nx + ny) // 2, bytes_accessed=64 * nx * ny, transcendentals=0
        ),
        name="first_parts",
    )(left, right, order_x, order_y, in_hbm(factors), start)


def depth_kernel(
    slot_ref, place_ref, left_hbm, right_hbm, factor_hbm, part_ref, speed_ref,
    keep_ref, send_ref, spectrum, real_ref, slow, state, columns, left_ref, right_ref, factor_ref, sems,
    *, total_freq,
):
    _, chips, depth_count, local_x, _ = speed_ref.shape
    power_count = factor_ref.shape[0]
    nx, ny = slow.shape
    image_scale = 1.0 / math.sqrt(total_freq)
    scale = (slot_ref[place_ref[0]] + 1).astype(jnp.float32) / total_freq
    core = lax.rem(place_ref[0], 2)

    def rows_of(chip, number):
        block = 2 * chip + number
        if 2 * chip >= chips:
            block = 3 * chips - 1 - block
        if isinstance(block, int):
            return slice(block * local_x, (block + 1) * local_x)
        return pl.ds(pl.multiple_of(block * local_x, local_x), local_x)

    def on_core(act):
        if local_x % SUBLANES == 0:
            act(core, 1 - core)
        else:
            for number in range(2):
                pl.when(core == number)(functools.partial(act, number, 1 - number))

    def load_slow(z):
        def act(own, other):
            for i, chip in enumerate(chip_order(chips)):
                slow[rows_of(chip, own), :] = scale / speed_ref[0, i, z].astype(jnp.float32)
                slow[rows_of(chip, other), :] = scale / speed_ref[1, i, z].astype(jnp.float32)

        on_core(act)

    def store_image(z):
        half = ny // 2

        def act(own, other):
            for i, chip in enumerate(chip_order(chips)):
                for side in range(2):
                    lanes = slice(side * half, (side + 1) * half)
                    keep_ref[i, 2 * z + side] = state[0, rows_of(chip, own), lanes] * image_scale
                    send_ref[i, 2 * z + side] = state[0, rows_of(chip, other), lanes] * image_scale

        on_core(act)

    sides = [
        pltpu.make_async_copy(right_hbm, right_ref, sems.at[0]),
        pltpu.make_async_copy(left_hbm, left_ref, sems.at[1]),
    ]
    fetch = pltpu.make_async_copy(factor_hbm, factor_ref, sems.at[2])
    for copy in sides:
        copy.start()
    fetch.start()
    load_slow(0)
    for c in range(2):
        total = part_ref[power_count - 1, c]
        for j in range(power_count - 2, -1, -1):
            total = total * slow[...] + part_ref[j, c]
        state[c] = total
    store_image(0)

    for copy in sides:
        copy.wait()

    for z in range(1, depth_count):
        last = z == depth_count - 1
        load_slow(z)
        for c in range(2):
            spectrum[c] = forward(state[c], left_ref, right_ref)
        if z == 1:
            fetch.wait()
        parts = range(1) if last else range(2)
        half_parts(left_ref, factor_ref, spectrum, columns, parts)
        sum_powers(right_ref, columns, slow, state, parts, CHUNK)
        store_image(z)
    real_ref[...] = state[0]
    shares = 2 * depth_count
    peak = jnp.max(jnp.abs(keep_ref[:, :shares]), axis=(0, 1))
    peak = jnp.maximum(peak, jnp.max(jnp.abs(send_ref[:, :shares]), axis=(0, 1)))
    peak = jnp.max(jnp.max(peak, axis=0, keepdims=True), axis=1, keepdims=True)
    for chip in range(chips):
        keep_ref[chip, shares] = jnp.broadcast_to(peak, keep_ref.shape[2:])
        send_ref[chip, shares] = jnp.broadcast_to(peak, keep_ref.shape[2:])


def depth_steps(freq_slot, place, left, right, factors, parts, speed):
    _, chips, depth_count, local_x, ny = speed.shape
    nx = factors.shape[2]

    def kernel(*refs):
        depth_kernel(*refs, total_freq=freq_slot.shape[0])

    share = jax.ShapeDtypeStruct((chips, 2 * depth_count + 1, local_x, ny // 2), jnp.float32)
    field = jax.ShapeDtypeStruct((nx, ny), jnp.float32)
    return pl.pallas_call(
        kernel,
        out_shape=(share, share, jax.ShapeDtypeStruct((2, nx, ny), jnp.float32), field, field),
        in_specs=[SMEM, SMEM, HBM, HBM, HBM, VMEM, VMEM],
        out_specs=(VMEM,) * 5,
        scratch_shapes=[
            pltpu.VMEM((2, nx, ny), jnp.float32),
            pltpu.VMEM(factors.shape, jnp.float32),
            pltpu.VMEM(left.shape, jnp.bfloat16),
            pltpu.VMEM(right.shape, jnp.bfloat16),
            pltpu.VMEM(factors.shape, jnp.float32),
            pltpu.SemaphoreType.DMA((3,)),
        ],
        compiler_params=pltpu.CompilerParams(vmem_limit_bytes=12 * 1024 * 1024),
        cost_estimate=pl.CostEstimate(
            flops=depth_count * 80 * nx * ny * (nx + ny) // 2, bytes_accessed=64 * nx * ny, transcendentals=0
        ),
        name="depth_steps",
    )(freq_slot, place, in_hbm(left), in_hbm(right), in_hbm(factors), in_vmem(parts), speed)


def last_kernel(
    left_hbm, right_hbm, order_x_hbm, order_y_hbm, factor_hbm, spectrum, real_ref, slow,
    field_ref, state, columns, left_ref, right_ref, order_x_ref, order_y_ref, factor_ref, sems,
):
    pairs = [
        (order_y_hbm, order_y_ref), (order_x_hbm, order_x_ref), (left_hbm, left_ref), (right_hbm, right_ref),
        (factor_hbm, factor_ref),
    ]
    copies = [pltpu.make_async_copy(source, target, sems.at[i]) for i, (source, target) in enumerate(pairs)]
    for copy in copies:
        copy.start()
    for copy in copies[:2]:
        copy.wait()
    field_ref[0] = reorder(real_ref[...], order_x_ref[...], order_y_ref[...])
    for copy in copies[2:]:
        copy.wait()
    half_parts(left_ref, factor_ref, spectrum, columns, range(1, 2))
    sum_powers(right_ref, columns, slow, state, range(1, 2), CHUNK)
    field_ref[1] = reorder(state[1], order_x_ref[...], order_y_ref[...])


def last_field(left, right, order_x, order_y, factors, spectrum, real, slow):
    _, nx, ny = spectrum.shape
    tables = [left, right, order_x, order_y, factors]
    return pl.pallas_call(
        last_kernel,
        out_shape=jax.ShapeDtypeStruct((2, nx, ny), jnp.float32),
        in_specs=[HBM] * 5 + [VMEM] * 3,
        out_specs=VMEM,
        scratch_shapes=[
            pltpu.VMEM((2, nx, ny), jnp.float32),
            pltpu.VMEM(factors.shape, jnp.float32),
            *(pltpu.VMEM(table.shape, table.dtype) for table in tables),
            pltpu.SemaphoreType.DMA((5,)),
        ],
        compiler_params=pltpu.CompilerParams(vmem_limit_bytes=14 * 1024 * 1024),
        cost_estimate=pl.CostEstimate(
            flops=40 * nx * ny * (nx + ny) // 2, bytes_accessed=64 * nx * ny, transcendentals=0
        ),
        name="last_field",
    )(*(in_hbm(table) for table in tables), spectrum, real, slow)


def spectra_kernel(
    slot_hbm, table_hbm, traces_hbm, speed_hbm, rows_hbm, lanes_hbm,
    out_ref, slot_ref, table_ref, traces_ref, speed_ref, rows_ref, lanes_ref, bins, sems,
):
    slots, _, local_x, ny = out_ref.shape
    chunk = max(local_x // 4, 1)
    pairs = [
        (table_hbm, table_ref), (slot_hbm, slot_ref), (speed_hbm, speed_ref), (lanes_hbm, lanes_ref),
        (rows_hbm, rows_ref),
    ]
    copies = [pltpu.make_async_copy(source, target, sems.at[i]) for i, (source, target) in enumerate(pairs)]
    small = len(copies)
    for i, x in enumerate(range(0, local_x, chunk)):
        part = pl.ds(x, chunk)
        copies.append(pltpu.make_async_copy(traces_hbm.at[part], traces_ref.at[part], sems.at[small + i]))
    for copy in copies:
        copy.start()
    for copy in copies[:small]:
        copy.wait()
    speed = dot(rows_ref[...], dot(speed_ref[...], lanes_ref[...]).astype(jnp.bfloat16))
    order = device_order(slots)
    for i, f in enumerate(order):
        out_ref[i, 2] = speed[f * local_x : (f + 1) * local_x]
    for i, x in enumerate(range(0, local_x, chunk)):
        copies[small + i].wait()
        rows = traces_ref[x : x + chunk].reshape(chunk * ny, traces_ref.shape[2])
        result = lax.dot_general(
            table_ref[...], rows, (((1,), (1,)), ((), ())), preferred_element_type=jnp.float32
        )
        for k in range(chunk):
            bins[:, x + k, :] = result[:, k * ny : (k + 1) * ny]
    for i, f in enumerate(order):
        for c in range(2):
            out_ref[i, c] = bins[2 * slot_ref[f] + c] * SPECTRA_SCALE


def position_spectra(freq_slot, traces, speed):
    local_x, ny, sample_count = traces.shape
    slots = freq_slot.shape[0]
    nx = speed.shape[0]
    index = np.arange(1, slots + 1)[:, None] * np.arange(sample_count)[None, :] % sample_count
    phases = index.astype(np.float32) * np.float32(2.0 * math.pi / sample_count)
    table = np.stack([np.cos(phases), -np.sin(phases)], axis=1) / np.float32(math.sqrt(sample_count))
    table = jnp.asarray(table.reshape(2 * slots, sample_count).astype(jnp.bfloat16))
    order = np.arange(nx).reshape(-1, local_x)
    order[order.shape[0] // 2 :] = order[order.shape[0] // 2 :, ::-1]
    rows = jnp.asarray(np.eye(nx)[order.reshape(-1)].astype(jnp.bfloat16))
    lanes = jnp.asarray(fold_matrix(ny))
    chunk = max(local_x // 4, 1)
    return pl.pallas_call(
        spectra_kernel,
        out_shape=jax.ShapeDtypeStruct((slots, 3, local_x, ny), jnp.float32),
        in_specs=[HBM] * 6,
        out_specs=VMEM,
        scratch_shapes=[
            pltpu.SMEM((slots,), jnp.int32),
            pltpu.VMEM((2 * slots, sample_count), jnp.bfloat16),
            pltpu.VMEM(traces.shape, jnp.bfloat16),
            pltpu.VMEM(speed.shape, jnp.bfloat16),
            pltpu.VMEM((nx, nx), jnp.bfloat16),
            pltpu.VMEM((ny, ny), jnp.bfloat16),
            pltpu.VMEM((2 * slots, local_x, ny), jnp.float32),
            pltpu.SemaphoreType.DMA((5 + local_x // chunk,)),
        ],
        compiler_params=pltpu.CompilerParams(vmem_limit_bytes=8 * 1024 * 1024),
        cost_estimate=pl.CostEstimate(
            flops=4 * slots * traces.size, bytes_accessed=2 * traces.size, transcendentals=0
        ),
        name="position_spectra",
    )(in_hbm(freq_slot), in_hbm(table), in_hbm(traces), in_hbm(speed), in_hbm(rows), in_hbm(lanes))


def exact_dot(a, b):
    return jnp.dot(a, b, preferred_element_type=jnp.float32, precision=lax.Precision.HIGHEST)


def image_kernel(place_ref, lanes_ref, rows_ref, share_ref, image_ref):
    depth_count, local_x, ny = image_ref.shape
    half = ny // 2
    total = jnp.sum(share_ref[:, : 2 * depth_count] * jnp.exp2(share_ref[:, 2 * depth_count :]), axis=0)
    turned = exact_dot(
        jnp.concatenate([total[2 * z + 1] for z in range(depth_count)], axis=0), lanes_ref[...]
    )
    image = jnp.concatenate(
        [jnp.concatenate([total[2 * z] for z in range(depth_count)], axis=0), turned], axis=1
    )
    upper = place_ref[0] >= share_ref.shape[0]

    @pl.when(upper)
    def _():
        image_ref[...] = exact_dot(rows_ref[...], image).reshape(image_ref.shape)

    @pl.when(jnp.logical_not(upper))
    def _():
        image_ref[...] = image.reshape(image_ref.shape)


def image_rows(place, shares):
    _, parts, local_x, half = shares.shape
    depth_count = parts // 2
    lanes = jnp.asarray(np.eye(half)[::-1], jnp.float32)
    rows = jnp.asarray(np.kron(np.eye(depth_count), np.eye(local_x)[::-1]), jnp.float32)
    return pl.pallas_call(
        image_kernel,
        out_shape=jax.ShapeDtypeStruct((depth_count, local_x, 2 * half), jnp.float32),
        in_specs=[SMEM, VMEM, VMEM, VMEM],
        out_specs=VMEM,
        compiler_params=pltpu.CompilerParams(vmem_limit_bytes=4 * 1024 * 1024),
        name="image_rows",
    )(place, lanes, rows, shares)


def swap_cores(array, count):
    return lax.ppermute(array, "freq", [(i, i ^ 1) for i in range(count)])


def on_device(traces, velocity, poly_coef, freq_slot, depth_owner):
    devices = lax.axis_size("freq")
    local_x, ny, _ = traces.shape
    nx = devices * local_x
    chips = devices // 2
    depth_count = depth_owner.shape[0]
    place = lax.axis_index("freq").astype(jnp.int32).reshape(1)
    order = device_order(devices)
    same_core = [[2 * chip + core for chip in chip_order(chips)] for core in range(2)]

    spectra = position_spectra(freq_slot, traces, velocity.reshape(nx, ny))
    received = lax.all_to_all(
        spectra.astype(jnp.float16),
        "freq",
        split_axis=0,
        concat_axis=0,
        tiled=True,
        axis_index_groups=[order],
    )
    received, poly_coef = lax.optimization_barrier((received, poly_coef))
    factors = spectral_factors(poly_coef, nx, ny)
    start = received[:, :2].transpose(1, 0, 2, 3).reshape(2, nx, ny).astype(jnp.float32) / SPECTRA_SCALE

    owned = (depth_owner[:, None] == jnp.asarray(order, jnp.int32)[None, :]).astype(jnp.bfloat16)
    by_rows = received[:, 2].astype(jnp.bfloat16).reshape(devices, local_x * ny)
    chosen = jnp.dot(owned, by_rows, preferred_element_type=jnp.float32).astype(jnp.bfloat16)
    chosen = jnp.broadcast_to(
        chosen.reshape(1, depth_count, local_x, ny), (chips, depth_count, local_x, ny)
    )
    mine = lax.all_to_all(
        chosen, "freq", split_axis=0, concat_axis=0, tiled=True, axis_index_groups=same_core
    )
    left = jnp.asarray(np.swapaxes(right_matrices(nx), 1, 2))
    right = jnp.asarray(right_matrices(ny))
    order_x, order_y = jnp.asarray(fold_matrix(nx)), jnp.asarray(fold_matrix(ny))
    arrived = (np.array(order)[:, None] * local_x + np.arange(local_x)).reshape(-1)
    parts = first_parts(left, right, jnp.asarray(fold_matrix(nx)[:, arrived]), order_y, factors, start)
    parts, mine = lax.optimization_barrier((parts, mine))
    speed = jnp.stack([mine, swap_cores(mine, devices)])
    keep, send, spectrum, real, slow = depth_steps(
        freq_slot, place, left, right, factors, parts, speed
    )

    total = keep + swap_cores(send, devices)
    power = jnp.ceil(jnp.log2(jnp.maximum(total[:, 2 * depth_count :], 1e-30)))
    packed = jnp.concatenate([total[:, : 2 * depth_count] * jnp.exp2(-power), power], axis=1)
    shares = lax.all_to_all(
        packed.astype(jnp.float16),
        "freq",
        split_axis=0,
        concat_axis=0,
        tiled=True,
        axis_index_groups=same_core,
    )
    wavefield = last_field(left, right, order_x, order_y, factors, spectrum, real, slow)
    shares, wavefield = lax.optimization_barrier((shares, wavefield))
    return (image_rows(place, shares.astype(jnp.float32)), wavefield[:, None])


def solution(mesh):
    return jax.shard_map(
        on_device,
        mesh=mesh,
        in_specs=(
            P(("group", "freq"), None, None),
            P(("group", "freq"), None, None),
            P(),
            P(),
            P("group"),
        ),
        out_specs=(P(None, ("group", "freq"), None), P(None, ("group", "freq"), None, None)),
        check_vma=False,
    )
```

```python
import functools
import math

import jax
import jax.numpy as jnp
import numpy as np
from jax import lax
from jax.experimental import pallas as pl
from jax.experimental.pallas import tpu as pltpu
from jax.sharding import PartitionSpec as P

SPECTRA_SCALE = 512.0
SUBLANES = 8
CHUNK = 128
SMEM = pl.BlockSpec(memory_space=pltpu.SMEM)
VMEM = pl.BlockSpec(memory_space=pltpu.VMEM)
HBM = pl.BlockSpec(memory_space=pltpu.HBM)


def device_order(devices):
    length = devices // 4
    along = list(range(length // 2, -1, -1)) + list(range(length // 2 + 1, length))
    return [4 * z + 2 * y + core for y in (1, 0) for z in along for core in (1, 0)]


def chip_order(chips):
    length = chips // 2
    along = list(range(length // 2, length)) + list(range(length // 2 - 1, -1, -1))
    return [2 * z + y for y in (0, 1) for z in along]


def in_vmem(array):
    return pltpu.with_memory_space_constraint(array, pltpu.VMEM)


def in_hbm(array):
    return pltpu.with_memory_space_constraint(array, pltpu.HBM)


def eigenvalues(size):
    values = 2.0 + 2.0 * np.cos(np.pi * np.arange(1, size + 1) / (size + 1))
    return np.concatenate([values[0::2], values[1::2]])


def folded_sines(size):
    index = np.arange(1, size + 1)
    matrix = np.sqrt(2.0 / (size + 1)) * np.sin(np.pi * np.outer(index, index) / (size + 1))
    return matrix[: size // 2, 0::2], matrix[: size // 2, 1::2]


def right_matrices(size):
    out = []
    even, odd = folded_sines(size)
    for matrix in (even, odd, even.T, odd.T):
        high = matrix.astype(jnp.bfloat16)
        low = (matrix - high.astype(np.float64)).astype(jnp.bfloat16)
        out.append(np.block([[high, low], [high, np.zeros_like(low)]]))
    return np.stack(out)


def fold_order(size):
    half = size // 2
    return np.concatenate([np.arange(half), np.arange(size - 1, half - 1, -1)])


def fold_matrix(size):
    return np.eye(size)[fold_order(size)].astype(jnp.bfloat16)


def split(values):
    high = values.astype(jnp.bfloat16)
    return high, (values - high.astype(jnp.float32)).astype(jnp.bfloat16)


def dot(a, b):
    return jnp.dot(a, b, preferred_element_type=jnp.float32)


def along_y(values, matrix):
    half = values.shape[1]
    both = dot(jnp.concatenate(split(values), axis=1), matrix)
    return both[:, :half] + both[:, half:]


def along_x(values, matrix):
    half = values.shape[0]
    both = dot(matrix, jnp.concatenate(split(values), axis=0))
    return both[:half] + both[half:]


def forward(values, left_ref, right_ref):
    half = values.shape[1] // 2
    a, b = values[:, :half], values[:, half:]
    values = jnp.concatenate([along_y(a + b, right_ref[0]), along_y(a - b, right_ref[1])], axis=1)
    half = values.shape[0] // 2
    a, b = values[:half], values[half:]
    return jnp.concatenate([along_x(a + b, left_ref[0]), along_x(a - b, left_ref[1])], axis=0)


def inverse_x(values, left_ref):
    half = values.shape[0] // 2
    even, odd = along_x(values[:half], left_ref[2]), along_x(values[half:], left_ref[3])
    return jnp.concatenate([even + odd, even - odd], axis=0)


def inverse_y(values, right_ref):
    half = values.shape[1] // 2
    even, odd = along_y(values[:, :half], right_ref[2]), along_y(values[:, half:], right_ref[3])
    return jnp.concatenate([even + odd, even - odd], axis=1)


def reorder(values, left, right):
    high, low = split(values)
    values = dot(high, right) + dot(low, right)
    high, low = split(values)
    return dot(left, high) + dot(left, low)


def half_parts(left_ref, factor_ref, spectrum, columns, parts):
    for j in range(factor_ref.shape[0]):
        for c in parts:
            if c == 0:
                mixed = factor_ref[j, 0] * spectrum[0] - factor_ref[j, 1] * spectrum[1]
            else:
                mixed = factor_ref[j, 0] * spectrum[1] + factor_ref[j, 1] * spectrum[0]
            columns[j, c] = inverse_x(mixed, left_ref)


def sum_powers(right_ref, columns, slow, state, parts, chunk):
    power_count, _, nx, ny = columns.shape
    half = ny // 2
    for c in parts:
        for first in range(0, nx, chunk):
            rows = slice(first, first + chunk)
            stacked = jnp.concatenate([columns[j, c, rows, :] for j in range(power_count)], axis=0)
            even, odd = along_y(stacked[:, :half], right_ref[2]), along_y(stacked[:, half:], right_ref[3])
            low, high = even + odd, even - odd
            for values, lanes in ((low, slice(0, half)), (high, slice(half, ny))):
                total = values[(power_count - 1) * chunk :]
                for j in range(power_count - 2, -1, -1):
                    total = total * slow[rows, lanes] + values[j * chunk : (j + 1) * chunk]
                state[c, rows, lanes] = total


def store_factors(coef_ref, lambda_x_ref, lambda_y_ref, factor_ref):
    term_count, power_count = coef_ref.shape[1:]
    block = 32

    def rows_step(i, carry):
        rows = pl.ds(pl.multiple_of(i * block, block), block)
        g = lambda_x_ref[rows, :] * lambda_y_ref[0:1, :] * 0.125 - 1.0
        twice = 2.0 * g
        sums = [[coef_ref[c, 0, j] + coef_ref[c, 1, j] * g for c in range(2)] for j in range(power_count)]
        before, now = jnp.ones_like(g), g
        for k in range(2, term_count):
            before, now = now, twice * now - before
            for j in range(power_count):
                for c in range(2):
                    sums[j][c] = sums[j][c] + coef_ref[c, k, j] * now
        for j in range(power_count):
            for c in range(2):
                factor_ref[j, c, rows, :] = sums[j][c]
        return carry

    lax.fori_loop(0, lambda_x_ref.shape[0] // block, rows_step, 0)


def first_kernel(
    coef_ref, lambda_x_ref, lambda_y_ref, left_hbm, right_hbm, order_x_hbm, order_y_hbm, start_ref,
    part_ref, factor_hbm, spectrum, columns, factor_ref, left_ref, right_ref, order_x_ref, order_y_ref, sems,
    *, arrival,
):
    rows = start_ref.shape[1] // len(arrival)
    pairs = [
        (left_hbm, left_ref), (right_hbm, right_ref), (order_x_hbm, order_x_ref), (order_y_hbm, order_y_ref),
        (factor_ref, factor_hbm),
    ]
    *fetches, put = [
        pltpu.make_async_copy(source, target, sems.at[i]) for i, (source, target) in enumerate(pairs)
    ]
    for fetch in fetches:
        fetch.start()
    store_factors(coef_ref, lambda_x_ref, lambda_y_ref, factor_ref)
    put.start()
    for fetch in fetches:
        fetch.wait()
    for c in range(2):
        natural = jnp.concatenate([start_ref[c, i * rows : (i + 1) * rows] for i in arrival], axis=0)
        spectrum[c] = forward(reorder(natural, order_x_ref[...], order_y_ref[...]), left_ref, right_ref)
    half_parts(left_ref, factor_ref, spectrum, columns, range(2))
    for j in range(part_ref.shape[0]):
        for c in range(2):
            part_ref[j, c] = inverse_y(columns[j, c], right_ref)
    put.wait()


def first_parts(poly_coef, left, right, order_x, order_y, start, arrival):
    _, nx, ny = start.shape
    shape = (poly_coef.shape[2], 2, nx, ny)
    tables = [left, right, order_x, order_y]

    def kernel(*refs):
        first_kernel(*refs, arrival=arrival)

    return pl.pallas_call(
        kernel,
        out_shape=(pltpu.VMEM(shape, jnp.float32), pltpu.HBM(shape, jnp.float32)),
        in_specs=[SMEM, VMEM, VMEM, HBM, HBM, HBM, HBM, VMEM],
        out_specs=(VMEM, HBM),
        scratch_shapes=[
            pltpu.VMEM((2, nx, ny), jnp.float32),
            pltpu.VMEM(shape, jnp.float32),
            pltpu.VMEM(shape, jnp.float32),
            *(pltpu.VMEM(table.shape, table.dtype) for table in tables),
            pltpu.SemaphoreType.DMA((5,)),
        ],
        compiler_params=pltpu.CompilerParams(vmem_limit_bytes=12 * 1024 * 1024),
        cost_estimate=pl.CostEstimate(
            flops=80 * nx * ny * (nx + ny) // 2, bytes_accessed=64 * nx * ny, transcendentals=0
        ),
        name="first_parts",
    )(
        poly_coef,
        jnp.asarray(eigenvalues(nx)[:, None], jnp.float32),
        jnp.asarray(eigenvalues(ny)[None, :], jnp.float32),
        *(in_hbm(table) for table in tables),
        start,
    )


def depth_kernel(
    slot_ref, place_ref, left_hbm, right_hbm, factor_hbm, part_ref, speed_ref,
    keep_ref, send_ref, spectrum, real_ref, slow, state, columns, left_ref, right_ref, factor_ref, sems,
    *, total_freq,
):
    _, chips, depth_count, local_x, _ = speed_ref.shape
    power_count = factor_ref.shape[0]
    nx, ny = slow.shape
    image_scale = 1.0 / math.sqrt(total_freq)
    scale = (slot_ref[place_ref[0]] + 1).astype(jnp.float32) / total_freq
    core = lax.rem(place_ref[0], 2)

    def rows_of(chip, number):
        block = 2 * chip + number
        if 2 * chip >= chips:
            block = 3 * chips - 1 - block
        if isinstance(block, int):
            return slice(block * local_x, (block + 1) * local_x)
        return pl.ds(pl.multiple_of(block * local_x, local_x), local_x)

    def on_core(act):
        if local_x % SUBLANES == 0:
            act(core, 1 - core)
        else:
            for number in range(2):
                pl.when(core == number)(functools.partial(act, number, 1 - number))

    def load_slow(z):
        def act(own, other):
            for i, chip in enumerate(chip_order(chips)):
                slow[rows_of(chip, own), :] = scale / speed_ref[0, i, z].astype(jnp.float32)
                slow[rows_of(chip, other), :] = scale / speed_ref[1, i, z].astype(jnp.float32)

        on_core(act)

    def store_image(z):
        half = ny // 2

        def act(own, other):
            for i, chip in enumerate(chip_order(chips)):
                for side in range(2):
                    lanes = slice(side * half, (side + 1) * half)
                    keep_ref[i, 2 * z + side] = state[0, rows_of(chip, own), lanes] * image_scale
                    send_ref[i, 2 * z + side] = state[0, rows_of(chip, other), lanes] * image_scale

        on_core(act)

    sides = [
        pltpu.make_async_copy(right_hbm, right_ref, sems.at[0]),
        pltpu.make_async_copy(left_hbm, left_ref, sems.at[1]),
    ]
    fetch = pltpu.make_async_copy(factor_hbm, factor_ref, sems.at[2])
    for copy in sides:
        copy.start()
    fetch.start()
    load_slow(0)
    for c in range(2):
        total = part_ref[power_count - 1, c]
        for j in range(power_count - 2, -1, -1):
            total = total * slow[...] + part_ref[j, c]
        state[c] = total
    store_image(0)

    for copy in sides:
        copy.wait()

    for z in range(1, depth_count):
        last = z == depth_count - 1
        load_slow(z)
        for c in range(2):
            spectrum[c] = forward(state[c], left_ref, right_ref)
        if z == 1:
            fetch.wait()
        parts = range(1) if last else range(2)
        half_parts(left_ref, factor_ref, spectrum, columns, parts)
        sum_powers(right_ref, columns, slow, state, parts, CHUNK)
        store_image(z)
    real_ref[...] = state[0]
    shares = 2 * depth_count
    peak = jnp.max(jnp.abs(keep_ref[:, :shares]), axis=(0, 1))
    peak = jnp.maximum(peak, jnp.max(jnp.abs(send_ref[:, :shares]), axis=(0, 1)))
    peak = jnp.max(jnp.max(peak, axis=0, keepdims=True), axis=1, keepdims=True)
    for chip in range(chips):
        keep_ref[chip, shares] = jnp.broadcast_to(peak, keep_ref.shape[2:])
        send_ref[chip, shares] = jnp.broadcast_to(peak, keep_ref.shape[2:])


def depth_steps(freq_slot, place, left, right, factors, parts, speed):
    _, chips, depth_count, local_x, ny = speed.shape
    nx = factors.shape[2]

    def kernel(*refs):
        depth_kernel(*refs, total_freq=freq_slot.shape[0])

    share = jax.ShapeDtypeStruct((chips, 2 * depth_count + 1, local_x, ny // 2), jnp.float32)
    field = jax.ShapeDtypeStruct((nx, ny), jnp.float32)
    return pl.pallas_call(
        kernel,
        out_shape=(share, share, jax.ShapeDtypeStruct((2, nx, ny), jnp.float32), field, field),
        in_specs=[SMEM, SMEM, HBM, HBM, HBM, VMEM, VMEM],
        out_specs=(VMEM,) * 5,
        scratch_shapes=[
            pltpu.VMEM((2, nx, ny), jnp.float32),
            pltpu.VMEM(factors.shape, jnp.float32),
            pltpu.VMEM(left.shape, jnp.bfloat16),
            pltpu.VMEM(right.shape, jnp.bfloat16),
            pltpu.VMEM(factors.shape, jnp.float32),
            pltpu.SemaphoreType.DMA((3,)),
        ],
        compiler_params=pltpu.CompilerParams(vmem_limit_bytes=12 * 1024 * 1024),
        cost_estimate=pl.CostEstimate(
            flops=depth_count * 80 * nx * ny * (nx + ny) // 2, bytes_accessed=64 * nx * ny, transcendentals=0
        ),
        name="depth_steps",
    )(freq_slot, place, in_hbm(left), in_hbm(right), in_hbm(factors), in_vmem(parts), speed)


def last_kernel(
    left_hbm, right_hbm, order_x_hbm, order_y_hbm, factor_hbm, spectrum, real_ref, slow,
    field_ref, state, columns, left_ref, right_ref, order_x_ref, order_y_ref, factor_ref, sems,
):
    pairs = [
        (order_y_hbm, order_y_ref), (order_x_hbm, order_x_ref), (left_hbm, left_ref), (right_hbm, right_ref),
        (factor_hbm, factor_ref),
    ]
    copies = [pltpu.make_async_copy(source, target, sems.at[i]) for i, (source, target) in enumerate(pairs)]
    for copy in copies:
        copy.start()
    for copy in copies[:2]:
        copy.wait()
    field_ref[0] = reorder(real_ref[...], order_x_ref[...], order_y_ref[...])
    for copy in copies[2:]:
        copy.wait()
    half_parts(left_ref, factor_ref, spectrum, columns, range(1, 2))
    sum_powers(right_ref, columns, slow, state, range(1, 2), CHUNK)
    field_ref[1] = reorder(state[1], order_x_ref[...], order_y_ref[...])


def last_field(left, right, order_x, order_y, factors, spectrum, real, slow):
    _, nx, ny = spectrum.shape
    tables = [left, right, order_x, order_y, factors]
    return pl.pallas_call(
        last_kernel,
        out_shape=jax.ShapeDtypeStruct((2, nx, ny), jnp.float32),
        in_specs=[HBM] * 5 + [VMEM] * 3,
        out_specs=VMEM,
        scratch_shapes=[
            pltpu.VMEM((2, nx, ny), jnp.float32),
            pltpu.VMEM(factors.shape, jnp.float32),
            *(pltpu.VMEM(table.shape, table.dtype) for table in tables),
            pltpu.SemaphoreType.DMA((5,)),
        ],
        compiler_params=pltpu.CompilerParams(vmem_limit_bytes=14 * 1024 * 1024),
        cost_estimate=pl.CostEstimate(
            flops=40 * nx * ny * (nx + ny) // 2, bytes_accessed=64 * nx * ny, transcendentals=0
        ),
        name="last_field",
    )(*(in_hbm(table) for table in tables), spectrum, real, slow)


def spectra_kernel(
    slot_hbm, table_hbm, traces_hbm, speed_hbm, rows_hbm, lanes_hbm,
    out_ref, slot_ref, table_ref, traces_ref, speed_ref, rows_ref, lanes_ref, bins, sems,
):
    slots, _, local_x, ny = out_ref.shape
    chunk = max(local_x // 4, 1)
    pairs = [
        (table_hbm, table_ref), (slot_hbm, slot_ref), (speed_hbm, speed_ref), (lanes_hbm, lanes_ref),
        (rows_hbm, rows_ref),
    ]
    copies = [pltpu.make_async_copy(source, target, sems.at[i]) for i, (source, target) in enumerate(pairs)]
    small = len(copies)
    for i, x in enumerate(range(0, local_x, chunk)):
        part = pl.ds(x, chunk)
        copies.append(pltpu.make_async_copy(traces_hbm.at[part], traces_ref.at[part], sems.at[small + i]))
    for copy in copies:
        copy.start()
    for copy in copies[:small]:
        copy.wait()
    speed = dot(rows_ref[...], dot(speed_ref[...], lanes_ref[...]).astype(jnp.bfloat16))
    order = device_order(slots)
    for i, f in enumerate(order):
        out_ref[i, 2] = speed[f * local_x : (f + 1) * local_x]
    for i, x in enumerate(range(0, local_x, chunk)):
        copies[small + i].wait()
        rows = traces_ref[x : x + chunk].reshape(chunk * ny, traces_ref.shape[2])
        result = lax.dot_general(
            table_ref[...], rows, (((1,), (1,)), ((), ())), preferred_element_type=jnp.float32
        )
        for k in range(chunk):
            bins[:, x + k, :] = result[:, k * ny : (k + 1) * ny]
    for i, f in enumerate(order):
        for c in range(2):
            out_ref[i, c] = bins[2 * slot_ref[f] + c] * SPECTRA_SCALE


def position_spectra(freq_slot, traces, speed):
    local_x, ny, sample_count = traces.shape
    slots = freq_slot.shape[0]
    nx = speed.shape[0]
    index = np.arange(1, slots + 1)[:, None] * np.arange(sample_count)[None, :] % sample_count
    phases = index.astype(np.float32) * np.float32(2.0 * math.pi / sample_count)
    table = np.stack([np.cos(phases), -np.sin(phases)], axis=1) / np.float32(math.sqrt(sample_count))
    table = jnp.asarray(table.reshape(2 * slots, sample_count).astype(jnp.bfloat16))
    order = np.arange(nx).reshape(-1, local_x)
    order[order.shape[0] // 2 :] = order[order.shape[0] // 2 :, ::-1]
    rows = jnp.asarray(np.eye(nx)[order.reshape(-1)].astype(jnp.bfloat16))
    lanes = jnp.asarray(fold_matrix(ny))
    chunk = max(local_x // 4, 1)
    return pl.pallas_call(
        spectra_kernel,
        out_shape=jax.ShapeDtypeStruct((slots, 3, local_x, ny), jnp.float32),
        in_specs=[HBM] * 6,
        out_specs=VMEM,
        scratch_shapes=[
            pltpu.SMEM((slots,), jnp.int32),
            pltpu.VMEM((2 * slots, sample_count), jnp.bfloat16),
            pltpu.VMEM(traces.shape, jnp.bfloat16),
            pltpu.VMEM(speed.shape, jnp.bfloat16),
            pltpu.VMEM((nx, nx), jnp.bfloat16),
            pltpu.VMEM((ny, ny), jnp.bfloat16),
            pltpu.VMEM((2 * slots, local_x, ny), jnp.float32),
            pltpu.SemaphoreType.DMA((5 + local_x // chunk,)),
        ],
        compiler_params=pltpu.CompilerParams(vmem_limit_bytes=8 * 1024 * 1024),
        cost_estimate=pl.CostEstimate(
            flops=4 * slots * traces.size, bytes_accessed=2 * traces.size, transcendentals=0
        ),
        name="position_spectra",
    )(in_hbm(freq_slot), in_hbm(table), in_hbm(traces), in_hbm(speed), in_hbm(rows), in_hbm(lanes))


def exact_dot(a, b):
    return jnp.dot(a, b, preferred_element_type=jnp.float32, precision=lax.Precision.HIGHEST)


def image_kernel(place_ref, lanes_ref, rows_ref, share_ref, image_ref):
    depth_count, local_x, ny = image_ref.shape
    half = ny // 2
    total = jnp.sum(share_ref[:, : 2 * depth_count] * jnp.exp2(share_ref[:, 2 * depth_count :]), axis=0)
    turned = exact_dot(
        jnp.concatenate([total[2 * z + 1] for z in range(depth_count)], axis=0), lanes_ref[...]
    )
    image = jnp.concatenate(
        [jnp.concatenate([total[2 * z] for z in range(depth_count)], axis=0), turned], axis=1
    )
    upper = place_ref[0] >= share_ref.shape[0]

    @pl.when(upper)
    def _():
        image_ref[...] = exact_dot(rows_ref[...], image).reshape(image_ref.shape)

    @pl.when(jnp.logical_not(upper))
    def _():
        image_ref[...] = image.reshape(image_ref.shape)


def image_rows(place, shares):
    _, parts, local_x, half = shares.shape
    depth_count = parts // 2
    lanes = jnp.asarray(np.eye(half)[::-1], jnp.float32)
    rows = jnp.asarray(np.kron(np.eye(depth_count), np.eye(local_x)[::-1]), jnp.float32)
    return pl.pallas_call(
        image_kernel,
        out_shape=jax.ShapeDtypeStruct((depth_count, local_x, 2 * half), jnp.float32),
        in_specs=[SMEM, VMEM, VMEM, VMEM],
        out_specs=VMEM,
        compiler_params=pltpu.CompilerParams(vmem_limit_bytes=4 * 1024 * 1024),
        name="image_rows",
    )(place, lanes, rows, shares)


def swap_cores(array, count):
    return lax.ppermute(array, "freq", [(i, i ^ 1) for i in range(count)])


def on_device(traces, velocity, poly_coef, freq_slot, depth_owner):
    devices = lax.axis_size("freq")
    local_x, ny, _ = traces.shape
    nx = devices * local_x
    chips = devices // 2
    depth_count = depth_owner.shape[0]
    place = lax.axis_index("freq").astype(jnp.int32).reshape(1)
    order = device_order(devices)
    same_core = [[2 * chip + core for chip in chip_order(chips)] for core in range(2)]

    spectra = position_spectra(freq_slot, traces, velocity.reshape(nx, ny))
    received = lax.all_to_all(
        spectra.astype(jnp.float16),
        "freq",
        split_axis=0,
        concat_axis=0,
        tiled=True,
        axis_index_groups=[order],
    )
    start = received[:, :2].transpose(1, 0, 2, 3).reshape(2, nx, ny).astype(jnp.float32) / SPECTRA_SCALE

    owned = (depth_owner[:, None] == jnp.asarray(order, jnp.int32)[None, :]).astype(jnp.bfloat16)
    by_rows = received[:, 2].astype(jnp.bfloat16).reshape(devices, local_x * ny)
    chosen = jnp.dot(owned, by_rows, preferred_element_type=jnp.float32).astype(jnp.bfloat16)
    chosen = jnp.broadcast_to(
        chosen.reshape(1, depth_count, local_x, ny), (chips, depth_count, local_x, ny)
    )
    mine = lax.all_to_all(
        chosen, "freq", split_axis=0, concat_axis=0, tiled=True, axis_index_groups=same_core
    )
    left = jnp.asarray(np.swapaxes(right_matrices(nx), 1, 2))
    right = jnp.asarray(right_matrices(ny))
    order_x, order_y = jnp.asarray(fold_matrix(nx)), jnp.asarray(fold_matrix(ny))
    arrival = [order.index(i) for i in range(devices)]
    parts, factors = first_parts(poly_coef, left, right, order_x, order_y, start, arrival)
    parts, mine = lax.optimization_barrier((parts, mine))
    speed = jnp.stack([mine, swap_cores(mine, devices)])
    keep, send, spectrum, real, slow = depth_steps(
        freq_slot, place, left, right, factors, parts, speed
    )

    total = keep + swap_cores(send, devices)
    power = jnp.ceil(jnp.log2(jnp.maximum(total[:, 2 * depth_count :], 1e-30)))
    packed = jnp.concatenate([total[:, : 2 * depth_count] * jnp.exp2(-power), power], axis=1)
    shares = lax.all_to_all(
        packed.astype(jnp.float16),
        "freq",
        split_axis=0,
        concat_axis=0,
        tiled=True,
        axis_index_groups=same_core,
    )
    wavefield = last_field(left, right, order_x, order_y, factors, spectrum, real, slow)
    shares, wavefield = lax.optimization_barrier((shares, wavefield))
    return (image_rows(place, shares.astype(jnp.float32)), wavefield[:, None])


def solution(mesh):
    return jax.shard_map(
        on_device,
        mesh=mesh,
        in_specs=(
            P(("group", "freq"), None, None),
            P(("group", "freq"), None, None),
            P(),
            P(),
            P("group"),
        ),
        out_specs=(P(None, ("group", "freq"), None), P(None, ("group", "freq"), None, None)),
        check_vma=False,
    )
```

```python
import functools
import math

import jax
import jax.numpy as jnp
import numpy as np
from jax import lax
from jax.experimental import pallas as pl
from jax.experimental.pallas import tpu as pltpu
from jax.sharding import PartitionSpec as P

SPECTRA_SCALE = 512.0
SUBLANES = 8
CHUNK = 128
SMEM = pl.BlockSpec(memory_space=pltpu.SMEM)
VMEM = pl.BlockSpec(memory_space=pltpu.VMEM)
HBM = pl.BlockSpec(memory_space=pltpu.HBM)


def device_order(devices):
    length = devices // 4
    along = list(range(length // 2, -1, -1)) + list(range(length // 2 + 1, length))
    return [4 * z + 2 * y + core for core in (1, 0) for z in along for y in (1, 0)]


def chip_order(chips):
    length = chips // 2
    along = list(range(length // 2, length)) + list(range(length // 2 - 1, -1, -1))
    return [2 * z + y for y in (0, 1) for z in along]


def in_vmem(array):
    return pltpu.with_memory_space_constraint(array, pltpu.VMEM)


def in_hbm(array):
    return pltpu.with_memory_space_constraint(array, pltpu.HBM)


def eigenvalues(size):
    values = 2.0 + 2.0 * np.cos(np.pi * np.arange(1, size + 1) / (size + 1))
    return np.concatenate([values[0::2], values[1::2]])


def folded_sines(size):
    index = np.arange(1, size + 1)
    matrix = np.sqrt(2.0 / (size + 1)) * np.sin(np.pi * np.outer(index, index) / (size + 1))
    return matrix[: size // 2, 0::2], matrix[: size // 2, 1::2]


def right_matrices(size):
    out = []
    even, odd = folded_sines(size)
    for matrix in (even, odd, even.T, odd.T):
        high = matrix.astype(jnp.bfloat16)
        low = (matrix - high.astype(np.float64)).astype(jnp.bfloat16)
        out.append(np.block([[high, low], [high, np.zeros_like(low)]]))
    return np.stack(out)


def fold_order(size):
    half = size // 2
    return np.concatenate([np.arange(half), np.arange(size - 1, half - 1, -1)])


def fold_matrix(size):
    return np.eye(size)[fold_order(size)].astype(jnp.bfloat16)


def split(values):
    high = values.astype(jnp.bfloat16)
    return high, (values - high.astype(jnp.float32)).astype(jnp.bfloat16)


def dot(a, b):
    return jnp.dot(a, b, preferred_element_type=jnp.float32)


def along_y(values, matrix):
    half = values.shape[1]
    both = dot(jnp.concatenate(split(values), axis=1), matrix)
    return both[:, :half] + both[:, half:]


def along_x(values, matrix):
    half = values.shape[0]
    both = dot(matrix, jnp.concatenate(split(values), axis=0))
    return both[:half] + both[half:]


def forward(values, left_ref, right_ref):
    half = values.shape[1] // 2
    a, b = values[:, :half], values[:, half:]
    values = jnp.concatenate([along_y(a + b, right_ref[0]), along_y(a - b, right_ref[1])], axis=1)
    half = values.shape[0] // 2
    a, b = values[:half], values[half:]
    return jnp.concatenate([along_x(a + b, left_ref[0]), along_x(a - b, left_ref[1])], axis=0)


def inverse_x(values, left_ref):
    half = values.shape[0] // 2
    even, odd = along_x(values[:half], left_ref[2]), along_x(values[half:], left_ref[3])
    return jnp.concatenate([even + odd, even - odd], axis=0)


def inverse_y(values, right_ref):
    half = values.shape[1] // 2
    even, odd = along_y(values[:, :half], right_ref[2]), along_y(values[:, half:], right_ref[3])
    return jnp.concatenate([even + odd, even - odd], axis=1)


def reorder(values, left, right):
    high, low = split(values)
    values = dot(high, right) + dot(low, right)
    high, low = split(values)
    return dot(left, high) + dot(left, low)


def half_parts(left_ref, factor_ref, spectrum, columns, parts):
    for j in range(factor_ref.shape[0]):
        for c in parts:
            if c == 0:
                mixed = factor_ref[j, 0] * spectrum[0] - factor_ref[j, 1] * spectrum[1]
            else:
                mixed = factor_ref[j, 0] * spectrum[1] + factor_ref[j, 1] * spectrum[0]
            columns[j, c] = inverse_x(mixed, left_ref)


def sum_powers(right_ref, columns, slow, state, parts, chunk):
    power_count, _, nx, ny = columns.shape
    half = ny // 2
    for c in parts:
        for first in range(0, nx, chunk):
            rows = slice(first, first + chunk)
            stacked = jnp.concatenate([columns[j, c, rows, :] for j in range(power_count)], axis=0)
            even, odd = along_y(stacked[:, :half], right_ref[2]), along_y(stacked[:, half:], right_ref[3])
            low, high = even + odd, even - odd
            for values, lanes in ((low, slice(0, half)), (high, slice(half, ny))):
                total = values[(power_count - 1) * chunk :]
                for j in range(power_count - 2, -1, -1):
                    total = total * slow[rows, lanes] + values[j * chunk : (j + 1) * chunk]
                state[c, rows, lanes] = total


def store_factors(coef_ref, lambda_x_ref, lambda_y_ref, factor_ref):
    term_count, power_count = coef_ref.shape[1:]
    block = 32

    def rows_step(i, carry):
        rows = pl.ds(pl.multiple_of(i * block, block), block)
        g = lambda_x_ref[rows, :] * lambda_y_ref[0:1, :] * 0.125 - 1.0
        twice = 2.0 * g
        sums = [[coef_ref[c, 0, j] + coef_ref[c, 1, j] * g for c in range(2)] for j in range(power_count)]
        before, now = jnp.ones_like(g), g
        for k in range(2, term_count):
            before, now = now, twice * now - before
            for j in range(power_count):
                for c in range(2):
                    sums[j][c] = sums[j][c] + coef_ref[c, k, j] * now
        for j in range(power_count):
            for c in range(2):
                factor_ref[j, c, rows, :] = sums[j][c]
        return carry

    lax.fori_loop(0, lambda_x_ref.shape[0] // block, rows_step, 0)


def first_kernel(
    coef_ref, lambda_x_ref, lambda_y_ref, left_hbm, right_hbm, order_x_hbm, order_y_hbm, start_ref,
    part_ref, factor_hbm, spectrum, columns, factor_ref, left_ref, right_ref, order_x_ref, order_y_ref, sems,
    *, arrival,
):
    rows = start_ref.shape[1] // len(arrival)
    pairs = [
        (left_hbm, left_ref), (right_hbm, right_ref), (order_x_hbm, order_x_ref), (order_y_hbm, order_y_ref),
        (factor_ref, factor_hbm),
    ]
    *fetches, put = [
        pltpu.make_async_copy(source, target, sems.at[i]) for i, (source, target) in enumerate(pairs)
    ]
    for fetch in fetches:
        fetch.start()
    store_factors(coef_ref, lambda_x_ref, lambda_y_ref, factor_ref)
    put.start()
    for fetch in fetches:
        fetch.wait()
    for c in range(2):
        natural = jnp.concatenate([start_ref[c, i * rows : (i + 1) * rows] for i in arrival], axis=0)
        spectrum[c] = forward(reorder(natural, order_x_ref[...], order_y_ref[...]), left_ref, right_ref)
    half_parts(left_ref, factor_ref, spectrum, columns, range(2))
    for j in range(part_ref.shape[0]):
        for c in range(2):
            part_ref[j, c] = inverse_y(columns[j, c], right_ref)
    put.wait()


def first_parts(poly_coef, left, right, order_x, order_y, start, arrival):
    _, nx, ny = start.shape
    shape = (poly_coef.shape[2], 2, nx, ny)
    tables = [left, right, order_x, order_y]

    def kernel(*refs):
        first_kernel(*refs, arrival=arrival)

    return pl.pallas_call(
        kernel,
        out_shape=(pltpu.VMEM(shape, jnp.float32), pltpu.HBM(shape, jnp.float32)),
        in_specs=[SMEM, VMEM, VMEM, HBM, HBM, HBM, HBM, VMEM],
        out_specs=(VMEM, HBM),
        scratch_shapes=[
            pltpu.VMEM((2, nx, ny), jnp.float32),
            pltpu.VMEM(shape, jnp.float32),
            pltpu.VMEM(shape, jnp.float32),
            *(pltpu.VMEM(table.shape, table.dtype) for table in tables),
            pltpu.SemaphoreType.DMA((5,)),
        ],
        compiler_params=pltpu.CompilerParams(vmem_limit_bytes=12 * 1024 * 1024),
        cost_estimate=pl.CostEstimate(
            flops=80 * nx * ny * (nx + ny) // 2, bytes_accessed=64 * nx * ny, transcendentals=0
        ),
        name="first_parts",
    )(
        poly_coef,
        jnp.asarray(eigenvalues(nx)[:, None], jnp.float32),
        jnp.asarray(eigenvalues(ny)[None, :], jnp.float32),
        *(in_hbm(table) for table in tables),
        start,
    )


def depth_kernel(
    slot_ref, place_ref, left_hbm, right_hbm, factor_hbm, part_ref, speed_ref,
    keep_ref, send_ref, spectrum, real_ref, slow, state, columns, left_ref, right_ref, factor_ref, sems,
    *, total_freq,
):
    _, chips, depth_count, local_x, _ = speed_ref.shape
    power_count = factor_ref.shape[0]
    nx, ny = slow.shape
    image_scale = 1.0 / math.sqrt(total_freq)
    scale = (slot_ref[place_ref[0]] + 1).astype(jnp.float32) / total_freq
    core = lax.rem(place_ref[0], 2)

    def rows_of(chip, number):
        block = 2 * chip + number
        if 2 * chip >= chips:
            block = 3 * chips - 1 - block
        if isinstance(block, int):
            return slice(block * local_x, (block + 1) * local_x)
        return pl.ds(pl.multiple_of(block * local_x, local_x), local_x)

    def on_core(act):
        if local_x % SUBLANES == 0:
            act(core, 1 - core)
        else:
            for number in range(2):
                pl.when(core == number)(functools.partial(act, number, 1 - number))

    def load_slow(z):
        def act(own, other):
            for i, chip in enumerate(chip_order(chips)):
                slow[rows_of(chip, own), :] = scale / speed_ref[0, i, z].astype(jnp.float32)
                slow[rows_of(chip, other), :] = scale / speed_ref[1, i, z].astype(jnp.float32)

        on_core(act)

    def store_image(z):
        half = ny // 2

        def act(own, other):
            for i, chip in enumerate(chip_order(chips)):
                for side in range(2):
                    lanes = slice(side * half, (side + 1) * half)
                    keep_ref[i, 2 * z + side] = state[0, rows_of(chip, own), lanes] * image_scale
                    send_ref[i, 2 * z + side] = state[0, rows_of(chip, other), lanes] * image_scale

        on_core(act)

    sides = [
        pltpu.make_async_copy(right_hbm, right_ref, sems.at[0]),
        pltpu.make_async_copy(left_hbm, left_ref, sems.at[1]),
    ]
    fetch = pltpu.make_async_copy(factor_hbm, factor_ref, sems.at[2])
    for copy in sides:
        copy.start()
    fetch.start()
    load_slow(0)
    for c in range(2):
        total = part_ref[power_count - 1, c]
        for j in range(power_count - 2, -1, -1):
            total = total * slow[...] + part_ref[j, c]
        state[c] = total
    store_image(0)

    for copy in sides:
        copy.wait()

    for z in range(1, depth_count):
        last = z == depth_count - 1
        load_slow(z)
        for c in range(2):
            spectrum[c] = forward(state[c], left_ref, right_ref)
        if z == 1:
            fetch.wait()
        parts = range(1) if last else range(2)
        half_parts(left_ref, factor_ref, spectrum, columns, parts)
        sum_powers(right_ref, columns, slow, state, parts, CHUNK)
        store_image(z)
    real_ref[...] = state[0]
    shares = 2 * depth_count
    peak = jnp.max(jnp.abs(keep_ref[:, :shares]), axis=(0, 1))
    peak = jnp.maximum(peak, jnp.max(jnp.abs(send_ref[:, :shares]), axis=(0, 1)))
    peak = jnp.max(jnp.max(peak, axis=0, keepdims=True), axis=1, keepdims=True)
    for chip in range(chips):
        keep_ref[chip, shares] = jnp.broadcast_to(peak, keep_ref.shape[2:])
        send_ref[chip, shares] = jnp.broadcast_to(peak, keep_ref.shape[2:])


def depth_steps(freq_slot, place, left, right, factors, parts, speed):
    _, chips, depth_count, local_x, ny = speed.shape
    nx = factors.shape[2]

    def kernel(*refs):
        depth_kernel(*refs, total_freq=freq_slot.shape[0])

    share = jax.ShapeDtypeStruct((chips, 2 * depth_count + 1, local_x, ny // 2), jnp.float32)
    field = jax.ShapeDtypeStruct((nx, ny), jnp.float32)
    return pl.pallas_call(
        kernel,
        out_shape=(share, share, jax.ShapeDtypeStruct((2, nx, ny), jnp.float32), field, field),
        in_specs=[SMEM, SMEM, HBM, HBM, HBM, VMEM, VMEM],
        out_specs=(VMEM,) * 5,
        scratch_shapes=[
            pltpu.VMEM((2, nx, ny), jnp.float32),
            pltpu.VMEM(factors.shape, jnp.float32),
            pltpu.VMEM(left.shape, jnp.bfloat16),
            pltpu.VMEM(right.shape, jnp.bfloat16),
            pltpu.VMEM(factors.shape, jnp.float32),
            pltpu.SemaphoreType.DMA((3,)),
        ],
        compiler_params=pltpu.CompilerParams(vmem_limit_bytes=12 * 1024 * 1024),
        cost_estimate=pl.CostEstimate(
            flops=depth_count * 80 * nx * ny * (nx + ny) // 2, bytes_accessed=64 * nx * ny, transcendentals=0
        ),
        name="depth_steps",
    )(freq_slot, place, in_hbm(left), in_hbm(right), in_hbm(factors), in_vmem(parts), speed)


def last_kernel(
    left_hbm, right_hbm, order_x_hbm, order_y_hbm, factor_hbm, spectrum, real_ref, slow,
    field_ref, state, columns, left_ref, right_ref, order_x_ref, order_y_ref, factor_ref, sems,
):
    pairs = [
        (order_y_hbm, order_y_ref), (order_x_hbm, order_x_ref), (left_hbm, left_ref), (right_hbm, right_ref),
        (factor_hbm, factor_ref),
    ]
    copies = [pltpu.make_async_copy(source, target, sems.at[i]) for i, (source, target) in enumerate(pairs)]
    for copy in copies:
        copy.start()
    for copy in copies[:2]:
        copy.wait()
    field_ref[0] = reorder(real_ref[...], order_x_ref[...], order_y_ref[...])
    for copy in copies[2:]:
        copy.wait()
    half_parts(left_ref, factor_ref, spectrum, columns, range(1, 2))
    sum_powers(right_ref, columns, slow, state, range(1, 2), CHUNK)
    field_ref[1] = reorder(state[1], order_x_ref[...], order_y_ref[...])


def last_field(left, right, order_x, order_y, factors, spectrum, real, slow):
    _, nx, ny = spectrum.shape
    tables = [left, right, order_x, order_y, factors]
    return pl.pallas_call(
        last_kernel,
        out_shape=jax.ShapeDtypeStruct((2, nx, ny), jnp.float32),
        in_specs=[HBM] * 5 + [VMEM] * 3,
        out_specs=VMEM,
        scratch_shapes=[
            pltpu.VMEM((2, nx, ny), jnp.float32),
            pltpu.VMEM(factors.shape, jnp.float32),
            *(pltpu.VMEM(table.shape, table.dtype) for table in tables),
            pltpu.SemaphoreType.DMA((5,)),
        ],
        compiler_params=pltpu.CompilerParams(vmem_limit_bytes=14 * 1024 * 1024),
        cost_estimate=pl.CostEstimate(
            flops=40 * nx * ny * (nx + ny) // 2, bytes_accessed=64 * nx * ny, transcendentals=0
        ),
        name="last_field",
    )(*(in_hbm(table) for table in tables), spectrum, real, slow)


def spectra_kernel(
    slot_hbm, table_hbm, traces_hbm, speed_hbm, rows_hbm, lanes_hbm,
    out_ref, slot_ref, table_ref, traces_ref, speed_ref, rows_ref, lanes_ref, bins, sems,
):
    slots, _, local_x, ny = out_ref.shape
    chunk = max(local_x // 2, 1)
    pairs = [
        (table_hbm, table_ref), (slot_hbm, slot_ref), (speed_hbm, speed_ref), (lanes_hbm, lanes_ref),
        (rows_hbm, rows_ref),
    ]
    copies = [pltpu.make_async_copy(source, target, sems.at[i]) for i, (source, target) in enumerate(pairs)]
    small = len(copies)
    for i, x in enumerate(range(0, local_x, chunk)):
        part = pl.ds(x, chunk)
        copies.append(pltpu.make_async_copy(traces_hbm.at[part], traces_ref.at[part], sems.at[small + i]))
    for copy in copies:
        copy.start()
    for copy in copies[:small]:
        copy.wait()
    speed = dot(rows_ref[...], dot(speed_ref[...], lanes_ref[...]).astype(jnp.bfloat16))
    order = device_order(slots)
    for i, f in enumerate(order):
        out_ref[i, 2] = speed[f * local_x : (f + 1) * local_x]
    for i, x in enumerate(range(0, local_x, chunk)):
        copies[small + i].wait()
        rows = traces_ref[x : x + chunk].reshape(chunk * ny, traces_ref.shape[2])
        result = lax.dot_general(
            table_ref[...], rows, (((1,), (1,)), ((), ())), preferred_element_type=jnp.float32
        )
        for k in range(chunk):
            bins[:, x + k, :] = result[:, k * ny : (k + 1) * ny]
    for i, f in enumerate(order):
        for c in range(2):
            out_ref[i, c] = bins[2 * slot_ref[f] + c] * SPECTRA_SCALE


def position_spectra(freq_slot, traces, speed):
    local_x, ny, sample_count = traces.shape
    slots = freq_slot.shape[0]
    nx = speed.shape[0]
    index = np.arange(1, slots + 1)[:, None] * np.arange(sample_count)[None, :] % sample_count
    phases = index.astype(np.float32) * np.float32(2.0 * math.pi / sample_count)
    table = np.stack([np.cos(phases), -np.sin(phases)], axis=1) / np.float32(math.sqrt(sample_count))
    table = jnp.asarray(table.reshape(2 * slots, sample_count).astype(jnp.bfloat16))
    order = np.arange(nx).reshape(-1, local_x)
    order[order.shape[0] // 2 :] = order[order.shape[0] // 2 :, ::-1]
    rows = jnp.asarray(np.eye(nx)[order.reshape(-1)].astype(jnp.bfloat16))
    lanes = jnp.asarray(fold_matrix(ny))
    chunk = max(local_x // 2, 1)
    return pl.pallas_call(
        spectra_kernel,
        out_shape=jax.ShapeDtypeStruct((slots, 3, local_x, ny), jnp.float32),
        in_specs=[HBM] * 6,
        out_specs=VMEM,
        scratch_shapes=[
            pltpu.SMEM((slots,), jnp.int32),
            pltpu.VMEM((2 * slots, sample_count), jnp.bfloat16),
            pltpu.VMEM(traces.shape, jnp.bfloat16),
            pltpu.VMEM(speed.shape, jnp.bfloat16),
            pltpu.VMEM((nx, nx), jnp.bfloat16),
            pltpu.VMEM((ny, ny), jnp.bfloat16),
            pltpu.VMEM((2 * slots, local_x, ny), jnp.float32),
            pltpu.SemaphoreType.DMA((5 + local_x // chunk,)),
        ],
        compiler_params=pltpu.CompilerParams(vmem_limit_bytes=8 * 1024 * 1024),
        cost_estimate=pl.CostEstimate(
            flops=4 * slots * traces.size, bytes_accessed=2 * traces.size, transcendentals=0
        ),
        name="position_spectra",
    )(in_hbm(freq_slot), in_hbm(table), in_hbm(traces), in_hbm(speed), in_hbm(rows), in_hbm(lanes))


def exact_dot(a, b):
    return jnp.dot(a, b, preferred_element_type=jnp.float32, precision=lax.Precision.HIGHEST)


def image_kernel(place_ref, lanes_ref, rows_ref, share_ref, image_ref):
    depth_count, local_x, ny = image_ref.shape
    half = ny // 2
    total = jnp.sum(share_ref[:, : 2 * depth_count] * jnp.exp2(share_ref[:, 2 * depth_count :]), axis=0)
    turned = exact_dot(
        jnp.concatenate([total[2 * z + 1] for z in range(depth_count)], axis=0), lanes_ref[...]
    )
    image = jnp.concatenate(
        [jnp.concatenate([total[2 * z] for z in range(depth_count)], axis=0), turned], axis=1
    )
    upper = place_ref[0] >= share_ref.shape[0]

    @pl.when(upper)
    def _():
        image_ref[...] = exact_dot(rows_ref[...], image).reshape(image_ref.shape)

    @pl.when(jnp.logical_not(upper))
    def _():
        image_ref[...] = image.reshape(image_ref.shape)


def image_rows(place, shares):
    _, parts, local_x, half = shares.shape
    depth_count = parts // 2
    lanes = jnp.asarray(np.eye(half)[::-1], jnp.float32)
    rows = jnp.asarray(np.kron(np.eye(depth_count), np.eye(local_x)[::-1]), jnp.float32)
    return pl.pallas_call(
        image_kernel,
        out_shape=jax.ShapeDtypeStruct((depth_count, local_x, 2 * half), jnp.float32),
        in_specs=[SMEM, VMEM, VMEM, VMEM],
        out_specs=VMEM,
        compiler_params=pltpu.CompilerParams(vmem_limit_bytes=4 * 1024 * 1024),
        name="image_rows",
    )(place, lanes, rows, shares)


def swap_cores(array, count):
    return lax.ppermute(array, "freq", [(i, i ^ 1) for i in range(count)])


def on_device(traces, velocity, poly_coef, freq_slot, depth_owner):
    devices = lax.axis_size("freq")
    local_x, ny, _ = traces.shape
    nx = devices * local_x
    chips = devices // 2
    depth_count = depth_owner.shape[0]
    place = lax.axis_index("freq").astype(jnp.int32).reshape(1)
    order = device_order(devices)
    same_core = [[2 * chip + core for chip in chip_order(chips)] for core in range(2)]

    spectra = position_spectra(freq_slot, traces, velocity.reshape(nx, ny))
    received = lax.all_to_all(
        spectra.astype(jnp.float16),
        "freq",
        split_axis=0,
        concat_axis=0,
        tiled=True,
        axis_index_groups=[order],
    )
    start = received[:, :2].transpose(1, 0, 2, 3).reshape(2, nx, ny).astype(jnp.float32) / SPECTRA_SCALE

    owned = (depth_owner[:, None] == jnp.asarray(order, jnp.int32)[None, :]).astype(jnp.bfloat16)
    by_rows = received[:, 2].astype(jnp.bfloat16).reshape(devices, local_x * ny)
    chosen = jnp.dot(owned, by_rows, preferred_element_type=jnp.float32).astype(jnp.bfloat16)
    chosen = jnp.broadcast_to(
        chosen.reshape(1, depth_count, local_x, ny), (chips, depth_count, local_x, ny)
    )
    mine = lax.all_to_all(
        chosen, "freq", split_axis=0, concat_axis=0, tiled=True, axis_index_groups=same_core
    )
    left = jnp.asarray(np.swapaxes(right_matrices(nx), 1, 2))
    right = jnp.asarray(right_matrices(ny))
    order_x, order_y = jnp.asarray(fold_matrix(nx)), jnp.asarray(fold_matrix(ny))
    arrival = [order.index(i) for i in range(devices)]
    parts, factors = first_parts(poly_coef, left, right, order_x, order_y, start, arrival)
    parts, mine = lax.optimization_barrier((parts, mine))
    speed = jnp.stack([mine, swap_cores(mine, devices)])
    keep, send, spectrum, real, slow = depth_steps(
        freq_slot, place, left, right, factors, parts, speed
    )

    total = keep + swap_cores(send, devices)
    power = jnp.ceil(jnp.log2(jnp.maximum(total[:, 2 * depth_count :], 1e-30)))
    packed = jnp.concatenate([total[:, : 2 * depth_count] * jnp.exp2(-power), power], axis=1)
    shares = lax.all_to_all(
        packed.astype(jnp.float16),
        "freq",
        split_axis=0,
        concat_axis=0,
        tiled=True,
        axis_index_groups=same_core,
    )
    wavefield = last_field(left, right, order_x, order_y, factors, spectrum, real, slow)
    shares, wavefield = lax.optimization_barrier((shares, wavefield))
    return (image_rows(place, shares.astype(jnp.float32)), wavefield[:, None])


def solution(mesh):
    return jax.shard_map(
        on_device,
        mesh=mesh,
        in_specs=(
            P(("group", "freq"), None, None),
            P(("group", "freq"), None, None),
            P(),
            P(),
            P("group"),
        ),
        out_specs=(P(None, ("group", "freq"), None), P(None, ("group", "freq"), None, None)),
        check_vma=False,
    )
```

```python
import functools
import math

import jax
import jax.numpy as jnp
import numpy as np
from jax import lax
from jax.experimental import pallas as pl
from jax.experimental.pallas import tpu as pltpu
from jax.sharding import PartitionSpec as P

SPECTRA_SCALE = 512.0
SUBLANES = 8
CHUNK = 128
SMEM = pl.BlockSpec(memory_space=pltpu.SMEM)
VMEM = pl.BlockSpec(memory_space=pltpu.VMEM)
HBM = pl.BlockSpec(memory_space=pltpu.HBM)


def device_order(devices):
    length = devices // 4
    along = list(range(length // 2, -1, -1)) + list(range(length // 2 + 1, length))
    return [4 * z + 2 * y + core for core in (1, 0) for z in along for y in (1, 0)]


def chip_order(chips):
    length = chips // 2
    along = list(range(length // 2, length)) + list(range(length // 2 - 1, -1, -1))
    return [2 * z + y for y in (0, 1) for z in along]


def in_vmem(array):
    return pltpu.with_memory_space_constraint(array, pltpu.VMEM)


def in_hbm(array):
    return pltpu.with_memory_space_constraint(array, pltpu.HBM)


def eigenvalues(size):
    values = 2.0 + 2.0 * np.cos(np.pi * np.arange(1, size + 1) / (size + 1))
    return np.concatenate([values[0::2], values[1::2]])


def folded_sines(size):
    index = np.arange(1, size + 1)
    matrix = np.sqrt(2.0 / (size + 1)) * np.sin(np.pi * np.outer(index, index) / (size + 1))
    return matrix[: size // 2, 0::2], matrix[: size // 2, 1::2]


def right_matrices(size):
    out = []
    even, odd = folded_sines(size)
    for matrix in (even, odd, even.T, odd.T):
        high = matrix.astype(jnp.bfloat16)
        low = (matrix - high.astype(np.float64)).astype(jnp.bfloat16)
        out.append(np.block([[high, low], [high, np.zeros_like(low)]]))
    return np.stack(out)


def fold_order(size):
    half = size // 2
    return np.concatenate([np.arange(half), np.arange(size - 1, half - 1, -1)])


def fold_matrix(size):
    return np.eye(size)[fold_order(size)].astype(jnp.bfloat16)


def split(values):
    high = values.astype(jnp.bfloat16)
    return high, (values - high.astype(jnp.float32)).astype(jnp.bfloat16)


def dot(a, b):
    return jnp.dot(a, b, preferred_element_type=jnp.float32)


def along_y(values, matrix):
    half = values.shape[1]
    both = dot(jnp.concatenate(split(values), axis=1), matrix)
    return both[:, :half] + both[:, half:]


def along_x(values, matrix):
    half = values.shape[0]
    both = dot(matrix, jnp.concatenate(split(values), axis=0))
    return both[:half] + both[half:]


def forward(values, left_ref, right_ref):
    half = values.shape[1] // 2
    a, b = values[:, :half], values[:, half:]
    values = jnp.concatenate([along_y(a + b, right_ref[0]), along_y(a - b, right_ref[1])], axis=1)
    half = values.shape[0] // 2
    a, b = values[:half], values[half:]
    return jnp.concatenate([along_x(a + b, left_ref[0]), along_x(a - b, left_ref[1])], axis=0)


def inverse_x(values, left_ref):
    half = values.shape[0] // 2
    even, odd = along_x(values[:half], left_ref[2]), along_x(values[half:], left_ref[3])
    return jnp.concatenate([even + odd, even - odd], axis=0)


def inverse_y(values, right_ref):
    half = values.shape[1] // 2
    even, odd = along_y(values[:, :half], right_ref[2]), along_y(values[:, half:], right_ref[3])
    return jnp.concatenate([even + odd, even - odd], axis=1)


def reorder(values, left, right):
    high, low = split(values)
    values = dot(high, right) + dot(low, right)
    high, low = split(values)
    return dot(left, high) + dot(left, low)


def half_parts(left_ref, factor_ref, spectrum, columns, parts):
    for j in range(factor_ref.shape[0]):
        for c in parts:
            if c == 0:
                mixed = factor_ref[j, 0] * spectrum[0] - factor_ref[j, 1] * spectrum[1]
            else:
                mixed = factor_ref[j, 0] * spectrum[1] + factor_ref[j, 1] * spectrum[0]
            columns[j, c] = inverse_x(mixed, left_ref)


def sum_powers(right_ref, columns, slow, state, parts, chunk):
    power_count, _, nx, ny = columns.shape
    half = ny // 2
    for c in parts:
        for first in range(0, nx, chunk):
            rows = slice(first, first + chunk)
            stacked = jnp.concatenate([columns[j, c, rows, :] for j in range(power_count)], axis=0)
            even, odd = along_y(stacked[:, :half], right_ref[2]), along_y(stacked[:, half:], right_ref[3])
            low, high = even + odd, even - odd
            for values, lanes in ((low, slice(0, half)), (high, slice(half, ny))):
                total = values[(power_count - 1) * chunk :]
                for j in range(power_count - 2, -1, -1):
                    total = total * slow[rows, lanes] + values[j * chunk : (j + 1) * chunk]
                state[c, rows, lanes] = total


def store_factors(coef_ref, lambda_x_ref, lambda_y_ref, factor_ref):
    term_count, power_count = coef_ref.shape[1:]
    block = 32

    def rows_step(i, carry):
        rows = pl.ds(pl.multiple_of(i * block, block), block)
        g = lambda_x_ref[rows, :] * lambda_y_ref[0:1, :] * 0.125 - 1.0
        twice = 2.0 * g
        sums = [[coef_ref[c, 0, j] + coef_ref[c, 1, j] * g for c in range(2)] for j in range(power_count)]
        before, now = jnp.ones_like(g), g
        for k in range(2, term_count):
            before, now = now, twice * now - before
            for j in range(power_count):
                for c in range(2):
                    sums[j][c] = sums[j][c] + coef_ref[c, k, j] * now
        for j in range(power_count):
            for c in range(2):
                factor_ref[j, c, rows, :] = sums[j][c]
        return carry

    lax.fori_loop(0, lambda_x_ref.shape[0] // block, rows_step, 0)


def first_kernel(
    coef_ref, lambda_x_ref, lambda_y_ref, left_hbm, right_hbm, order_x_hbm, order_y_hbm, start_ref,
    part_ref, factor_hbm, spectrum, columns, factor_ref, left_ref, right_ref, order_x_ref, order_y_ref, sems,
    *, arrival,
):
    rows = start_ref.shape[1] // len(arrival)
    pairs = [
        (left_hbm, left_ref), (right_hbm, right_ref), (order_x_hbm, order_x_ref), (order_y_hbm, order_y_ref),
        (factor_ref, factor_hbm),
    ]
    *fetches, put = [
        pltpu.make_async_copy(source, target, sems.at[i]) for i, (source, target) in enumerate(pairs)
    ]
    for fetch in fetches:
        fetch.start()
    store_factors(coef_ref, lambda_x_ref, lambda_y_ref, factor_ref)
    put.start()
    for fetch in fetches:
        fetch.wait()
    for c in range(2):
        natural = jnp.concatenate([start_ref[c, i * rows : (i + 1) * rows] for i in arrival], axis=0)
        spectrum[c] = forward(reorder(natural, order_x_ref[...], order_y_ref[...]), left_ref, right_ref)
    half_parts(left_ref, factor_ref, spectrum, columns, range(2))
    for j in range(part_ref.shape[0]):
        for c in range(2):
            part_ref[j, c] = inverse_y(columns[j, c], right_ref)
    put.wait()


def first_parts(poly_coef, left, right, order_x, order_y, start, arrival):
    _, nx, ny = start.shape
    shape = (poly_coef.shape[2], 2, nx, ny)
    tables = [left, right, order_x, order_y]

    def kernel(*refs):
        first_kernel(*refs, arrival=arrival)

    return pl.pallas_call(
        kernel,
        out_shape=(pltpu.VMEM(shape, jnp.float32), pltpu.HBM(shape, jnp.float32)),
        in_specs=[SMEM, VMEM, VMEM, HBM, HBM, HBM, HBM, VMEM],
        out_specs=(VMEM, HBM),
        scratch_shapes=[
            pltpu.VMEM((2, nx, ny), jnp.float32),
            pltpu.VMEM(shape, jnp.float32),
            pltpu.VMEM(shape, jnp.float32),
            *(pltpu.VMEM(table.shape, table.dtype) for table in tables),
            pltpu.SemaphoreType.DMA((5,)),
        ],
        compiler_params=pltpu.CompilerParams(vmem_limit_bytes=12 * 1024 * 1024),
        cost_estimate=pl.CostEstimate(
            flops=80 * nx * ny * (nx + ny) // 2, bytes_accessed=64 * nx * ny, transcendentals=0
        ),
        name="first_parts",
    )(
        poly_coef,
        jnp.asarray(eigenvalues(nx)[:, None], jnp.float32),
        jnp.asarray(eigenvalues(ny)[None, :], jnp.float32),
        *(in_hbm(table) for table in tables),
        start,
    )


def depth_kernel(
    slot_ref, place_ref, left_hbm, right_hbm, factor_hbm, part_ref, speed_ref,
    keep_ref, send_ref, spectrum, real_ref, slow, state, columns, left_ref, right_ref, factor_ref, sems,
    *, total_freq,
):
    _, chips, depth_count, local_x, _ = speed_ref.shape
    power_count = factor_ref.shape[0]
    nx, ny = slow.shape
    image_scale = 1.0 / math.sqrt(total_freq)
    scale = (slot_ref[place_ref[0]] + 1).astype(jnp.float32) / total_freq
    core = lax.rem(place_ref[0], 2)

    def rows_of(chip, number):
        block = 2 * chip + number
        if 2 * chip >= chips:
            block = 3 * chips - 1 - block
        if isinstance(block, int):
            return slice(block * local_x, (block + 1) * local_x)
        return pl.ds(pl.multiple_of(block * local_x, local_x), local_x)

    def on_core(act):
        if local_x % SUBLANES == 0:
            act(core, 1 - core)
        else:
            for number in range(2):
                pl.when(core == number)(functools.partial(act, number, 1 - number))

    def load_slow(z):
        def act(own, other):
            for i, chip in enumerate(chip_order(chips)):
                slow[rows_of(chip, own), :] = scale / speed_ref[0, i, z].astype(jnp.float32)
                slow[rows_of(chip, other), :] = scale / speed_ref[1, i, z].astype(jnp.float32)

        on_core(act)

    def store_image(z):
        half = ny // 2

        def act(own, other):
            for i, chip in enumerate(chip_order(chips)):
                for side in range(2):
                    lanes = slice(side * half, (side + 1) * half)
                    keep_ref[i, 2 * z + side] = state[0, rows_of(chip, own), lanes] * image_scale
                    send_ref[i, 2 * z + side] = state[0, rows_of(chip, other), lanes] * image_scale

        on_core(act)

    sides = [
        pltpu.make_async_copy(right_hbm, right_ref, sems.at[0]),
        pltpu.make_async_copy(left_hbm, left_ref, sems.at[1]),
    ]
    fetch = pltpu.make_async_copy(factor_hbm, factor_ref, sems.at[2])
    for copy in sides:
        copy.start()
    fetch.start()
    load_slow(0)
    for c in range(2):
        total = part_ref[power_count - 1, c]
        for j in range(power_count - 2, -1, -1):
            total = total * slow[...] + part_ref[j, c]
        state[c] = total
    store_image(0)

    for copy in sides:
        copy.wait()

    for z in range(1, depth_count):
        last = z == depth_count - 1
        load_slow(z)
        for c in range(2):
            spectrum[c] = forward(state[c], left_ref, right_ref)
        if z == 1:
            fetch.wait()
        parts = range(1) if last else range(2)
        half_parts(left_ref, factor_ref, spectrum, columns, parts)
        sum_powers(right_ref, columns, slow, state, parts, CHUNK)
        store_image(z)
    real_ref[...] = state[0]
    shares = 2 * depth_count
    peak = jnp.max(jnp.abs(keep_ref[:, :shares]), axis=(0, 1))
    peak = jnp.maximum(peak, jnp.max(jnp.abs(send_ref[:, :shares]), axis=(0, 1)))
    peak = jnp.max(jnp.max(peak, axis=0, keepdims=True), axis=1, keepdims=True)
    for chip in range(chips):
        keep_ref[chip, shares] = jnp.broadcast_to(peak, keep_ref.shape[2:])
        send_ref[chip, shares] = jnp.broadcast_to(peak, keep_ref.shape[2:])


def depth_steps(freq_slot, place, left, right, factors, parts, speed):
    _, chips, depth_count, local_x, ny = speed.shape
    nx = factors.shape[2]

    def kernel(*refs):
        depth_kernel(*refs, total_freq=freq_slot.shape[0])

    share = jax.ShapeDtypeStruct((chips, 2 * depth_count + 1, local_x, ny // 2), jnp.float32)
    field = jax.ShapeDtypeStruct((nx, ny), jnp.float32)
    return pl.pallas_call(
        kernel,
        out_shape=(share, share, jax.ShapeDtypeStruct((2, nx, ny), jnp.float32), field, field),
        in_specs=[SMEM, SMEM, HBM, HBM, HBM, VMEM, VMEM],
        out_specs=(VMEM,) * 5,
        scratch_shapes=[
            pltpu.VMEM((2, nx, ny), jnp.float32),
            pltpu.VMEM(factors.shape, jnp.float32),
            pltpu.VMEM(left.shape, jnp.bfloat16),
            pltpu.VMEM(right.shape, jnp.bfloat16),
            pltpu.VMEM(factors.shape, jnp.float32),
            pltpu.SemaphoreType.DMA((3,)),
        ],
        compiler_params=pltpu.CompilerParams(vmem_limit_bytes=12 * 1024 * 1024),
        cost_estimate=pl.CostEstimate(
            flops=depth_count * 80 * nx * ny * (nx + ny) // 2, bytes_accessed=64 * nx * ny, transcendentals=0
        ),
        name="depth_steps",
    )(freq_slot, place, in_hbm(left), in_hbm(right), in_hbm(factors), in_vmem(parts), speed)


def last_kernel(
    left_hbm, right_hbm, order_x_hbm, order_y_hbm, factor_hbm, spectrum, real_ref, slow,
    field_ref, state, columns, left_ref, right_ref, order_x_ref, order_y_ref, factor_ref, sems,
):
    pairs = [
        (order_y_hbm, order_y_ref), (order_x_hbm, order_x_ref), (left_hbm, left_ref), (right_hbm, right_ref),
        (factor_hbm, factor_ref),
    ]
    copies = [pltpu.make_async_copy(source, target, sems.at[i]) for i, (source, target) in enumerate(pairs)]
    for copy in copies:
        copy.start()
    for copy in copies[:2]:
        copy.wait()
    field_ref[0] = reorder(real_ref[...], order_x_ref[...], order_y_ref[...])
    for copy in copies[2:]:
        copy.wait()
    half_parts(left_ref, factor_ref, spectrum, columns, range(1, 2))
    sum_powers(right_ref, columns, slow, state, range(1, 2), CHUNK)
    field_ref[1] = reorder(state[1], order_x_ref[...], order_y_ref[...])


def last_field(left, right, order_x, order_y, factors, spectrum, real, slow):
    _, nx, ny = spectrum.shape
    tables = [left, right, order_x, order_y, factors]
    return pl.pallas_call(
        last_kernel,
        out_shape=jax.ShapeDtypeStruct((2, nx, ny), jnp.float32),
        in_specs=[HBM] * 5 + [VMEM] * 3,
        out_specs=VMEM,
        scratch_shapes=[
            pltpu.VMEM((2, nx, ny), jnp.float32),
            pltpu.VMEM(factors.shape, jnp.float32),
            *(pltpu.VMEM(table.shape, table.dtype) for table in tables),
            pltpu.SemaphoreType.DMA((5,)),
        ],
        compiler_params=pltpu.CompilerParams(vmem_limit_bytes=14 * 1024 * 1024),
        cost_estimate=pl.CostEstimate(
            flops=40 * nx * ny * (nx + ny) // 2, bytes_accessed=64 * nx * ny, transcendentals=0
        ),
        name="last_field",
    )(*(in_hbm(table) for table in tables), spectrum, real, slow)


def spectra_kernel(
    slot_hbm, table_hbm, traces_hbm, speed_hbm, rows_hbm, lanes_hbm,
    out_ref, slot_ref, table_ref, traces_ref, speed_ref, rows_ref, lanes_ref, bins, sems,
):
    slots, _, local_x, ny = out_ref.shape
    chunk = max(local_x // 2, 1)
    pairs = [
        (table_hbm, table_ref), (slot_hbm, slot_ref), (speed_hbm, speed_ref), (lanes_hbm, lanes_ref),
        (rows_hbm, rows_ref),
    ]
    copies = [pltpu.make_async_copy(source, target, sems.at[i]) for i, (source, target) in enumerate(pairs)]
    small = len(copies)
    for i, x in enumerate(range(0, local_x, chunk)):
        part = pl.ds(x, chunk)
        copies.append(pltpu.make_async_copy(traces_hbm.at[part], traces_ref.at[part], sems.at[small + i]))
    for copy in copies:
        copy.start()
    for copy in copies[:small]:
        copy.wait()
    speed = dot(rows_ref[...], dot(speed_ref[...], lanes_ref[...]).astype(jnp.bfloat16))
    order = device_order(slots)
    for i, f in enumerate(order):
        out_ref[i, 2] = speed[f * local_x : (f + 1) * local_x]
    for i, x in enumerate(range(0, local_x, chunk)):
        copies[small + i].wait()
        rows = traces_ref[x : x + chunk].reshape(chunk * ny, traces_ref.shape[2])
        result = lax.dot_general(
            table_ref[...], rows, (((1,), (1,)), ((), ())), preferred_element_type=jnp.float32
        )
        for k in range(chunk):
            bins[:, x + k, :] = result[:, k * ny : (k + 1) * ny]
    for i, f in enumerate(order):
        for c in range(2):
            out_ref[i, c] = bins[2 * slot_ref[f] + c] * SPECTRA_SCALE


def position_spectra(freq_slot, traces, speed):
    local_x, ny, sample_count = traces.shape
    slots = freq_slot.shape[0]
    nx = speed.shape[0]
    index = np.arange(1, slots + 1)[:, None] * np.arange(sample_count)[None, :] % sample_count
    phases = index.astype(np.float32) * np.float32(2.0 * math.pi / sample_count)
    table = np.stack([np.cos(phases), -np.sin(phases)], axis=1) / np.float32(math.sqrt(sample_count))
    table = jnp.asarray(table.reshape(2 * slots, sample_count).astype(jnp.bfloat16))
    order = np.arange(nx).reshape(-1, local_x)
    order[order.shape[0] // 2 :] = order[order.shape[0] // 2 :, ::-1]
    rows = jnp.asarray(np.eye(nx)[order.reshape(-1)].astype(jnp.bfloat16))
    lanes = jnp.asarray(fold_matrix(ny))
    chunk = max(local_x // 2, 1)
    return pl.pallas_call(
        spectra_kernel,
        out_shape=jax.ShapeDtypeStruct((slots, 3, local_x, ny), jnp.float32),
        in_specs=[HBM] * 6,
        out_specs=VMEM,
        scratch_shapes=[
            pltpu.SMEM((slots,), jnp.int32),
            pltpu.VMEM((2 * slots, sample_count), jnp.bfloat16),
            pltpu.VMEM(traces.shape, jnp.bfloat16),
            pltpu.VMEM(speed.shape, jnp.bfloat16),
            pltpu.VMEM((nx, nx), jnp.bfloat16),
            pltpu.VMEM((ny, ny), jnp.bfloat16),
            pltpu.VMEM((2 * slots, local_x, ny), jnp.float32),
            pltpu.SemaphoreType.DMA((5 + local_x // chunk,)),
        ],
        compiler_params=pltpu.CompilerParams(vmem_limit_bytes=8 * 1024 * 1024),
        cost_estimate=pl.CostEstimate(
            flops=4 * slots * traces.size, bytes_accessed=2 * traces.size, transcendentals=0
        ),
        name="position_spectra",
    )(in_hbm(freq_slot), in_hbm(table), in_hbm(traces), in_hbm(speed), in_hbm(rows), in_hbm(lanes))


def exact_dot(a, b):
    return jnp.dot(a, b, preferred_element_type=jnp.float32, precision=lax.Precision.HIGHEST)


def image_kernel(place_ref, lanes_ref, rows_ref, share_ref, image_ref):
    depth_count, local_x, ny = image_ref.shape
    half = ny // 2
    total = jnp.sum(share_ref[:, : 2 * depth_count] * jnp.exp2(share_ref[:, 2 * depth_count :]), axis=0)
    turned = exact_dot(
        jnp.concatenate([total[2 * z + 1] for z in range(depth_count)], axis=0), lanes_ref[...]
    )
    image = jnp.concatenate(
        [jnp.concatenate([total[2 * z] for z in range(depth_count)], axis=0), turned], axis=1
    )
    upper = place_ref[0] >= share_ref.shape[0]

    @pl.when(upper)
    def _():
        image_ref[...] = exact_dot(rows_ref[...], image).reshape(image_ref.shape)

    @pl.when(jnp.logical_not(upper))
    def _():
        image_ref[...] = image.reshape(image_ref.shape)


def image_rows(place, shares):
    _, parts, local_x, half = shares.shape
    depth_count = parts // 2
    lanes = jnp.asarray(np.eye(half)[::-1], jnp.float32)
    rows = jnp.asarray(np.kron(np.eye(depth_count), np.eye(local_x)[::-1]), jnp.float32)
    return pl.pallas_call(
        image_kernel,
        out_shape=jax.ShapeDtypeStruct((depth_count, local_x, 2 * half), jnp.float32),
        in_specs=[SMEM, VMEM, VMEM, VMEM],
        out_specs=VMEM,
        compiler_params=pltpu.CompilerParams(vmem_limit_bytes=4 * 1024 * 1024),
        name="image_rows",
    )(place, lanes, rows, shares)


def swap_cores(array, count):
    return lax.ppermute(array, "freq", [(i, i ^ 1) for i in range(count)])


def on_device(traces, velocity, poly_coef, freq_slot, depth_owner):
    devices = lax.axis_size("freq")
    local_x, ny, _ = traces.shape
    nx = devices * local_x
    chips = devices // 2
    depth_count = depth_owner.shape[0]
    place = lax.axis_index("freq").astype(jnp.int32).reshape(1)
    order = device_order(devices)
    same_core = [[2 * chip + core for chip in chip_order(chips)] for core in range(2)]

    spectra = position_spectra(freq_slot, traces, velocity.reshape(nx, ny))
    received = lax.all_to_all(
        spectra.astype(jnp.float16),
        "freq",
        split_axis=0,
        concat_axis=0,
        tiled=True,
        axis_index_groups=[order],
    )
    start = received[:, :2].transpose(1, 0, 2, 3).reshape(2, nx, ny).astype(jnp.float32) / SPECTRA_SCALE

    owned = (depth_owner[:, None] == jnp.asarray(order, jnp.int32)[None, :]).astype(jnp.bfloat16)
    by_rows = received[:, 2].astype(jnp.bfloat16).reshape(devices, local_x * ny)
    chosen = jnp.dot(owned, by_rows, preferred_element_type=jnp.float32).astype(jnp.bfloat16)
    chosen = jnp.broadcast_to(
        chosen.reshape(1, depth_count, local_x, ny), (chips, depth_count, local_x, ny)
    )
    mine = lax.all_to_all(
        chosen, "freq", split_axis=0, concat_axis=0, tiled=True, axis_index_groups=same_core
    )
    left = jnp.asarray(np.swapaxes(right_matrices(nx), 1, 2))
    right = jnp.asarray(right_matrices(ny))
    order_x, order_y = jnp.asarray(fold_matrix(nx)), jnp.asarray(fold_matrix(ny))
    arrival = [order.index(i) for i in range(devices)]
    parts, factors = first_parts(poly_coef, left, right, order_x, order_y, start, arrival)
    parts, mine = lax.optimization_barrier((parts, mine))
    speed = jnp.stack([mine, swap_cores(mine, devices)])
    keep, send, spectrum, real, slow = depth_steps(
        freq_slot, place, left, right, factors, parts, speed
    )

    parts_end = 2 * depth_count

    def pack(values, peak):
        power = jnp.ceil(jnp.log2(jnp.maximum(peak, 1e-30)))
        return jnp.concatenate([values * jnp.exp2(-power), power], axis=1).astype(jnp.float16)

    swapped = swap_cores(pack(send[:, :parts_end], send[:, parts_end:]), devices).astype(jnp.float32)
    peer_scale = jnp.exp2(swapped[:, parts_end:])
    packed = pack(
        keep[:, :parts_end] + swapped[:, :parts_end] * peer_scale, keep[:, parts_end:] + peer_scale
    )
    shares = lax.all_to_all(
        packed,
        "freq",
        split_axis=0,
        concat_axis=0,
        tiled=True,
        axis_index_groups=same_core,
    )
    wavefield = last_field(left, right, order_x, order_y, factors, spectrum, real, slow)
    shares, wavefield = lax.optimization_barrier((shares, wavefield))
    return (image_rows(place, shares.astype(jnp.float32)), wavefield[:, None])


def solution(mesh):
    return jax.shard_map(
        on_device,
        mesh=mesh,
        in_specs=(
            P(("group", "freq"), None, None),
            P(("group", "freq"), None, None),
            P(),
            P(),
            P("group"),
        ),
        out_specs=(P(None, ("group", "freq"), None), P(None, ("group", "freq"), None, None)),
        check_vma=False,
    )
```
